512 devices in a mesh: depth: 64 (over z_lo, y, core), chan: 8 (over x, z_hi).
Axes of the slice: x: 4, y: 4, z: 16 (z_hi: 2, z_lo: 8; z = z_hi * 8 + z_lo), core: 2. Of those that a mesh axis runs over, the one named last changes fastest.
Arguments:
- sample: bfloat16 [128, 128, 16, 128], P('chan', 'depth'), may hold values from -6 to 6
- first_weight: bfloat16 [256, 3456], P('chan'), may hold values from -0.109375 to 0.109375
- second_weight: bfloat16 [256, 6912], P('chan'), may hold values from -0.078125 to 0.078125
- cotangent: bfloat16 [256, 64, 8, 64], P('chan', 'depth'), may hold values from -0.023925781 to 0.023925781
Outputs:
- second_out: bfloat16 [256, 64, 8, 64], P('chan', 'depth')
- first_grad: float32 [256, 3456], P('chan', 'depth')
- second_grad: float32 [256, 6912], P('chan', 'depth')
The draws below stay inside these ranges and needn't reach their ends.
All inputs are finite; a program needn't handle non-finite values.
Results may differ from the reference program's by a relative error of at most 0.017.
Values may be sent and summed in bfloat16 or wider, within the bound.
A program may use at most 64 MiB of HBM per device.

```python
import jax
import jax.numpy as jnp
from jax import lax

CIN = 128
CMID = 256
HIN = 16
WIN = 128
DIN = 128
DOUT = 64
HO = 8
WO = 64


def levels(key, dims, cuts, least, top_value):
    def one(position, parts):
        heights = jax.random.uniform(jax.random.fold_in(jax.random.fold_in(key, 6), position), (parts,), jnp.float32, least / len(cuts), top_value / len(cuts))
        return jnp.repeat(jnp.exp(heights), dims[position] // parts).reshape((-1,) + (1,) * (len(dims) - position - 1))

    level = one(*cuts[0])
    for cut in cuts[1:]:
        level = level * one(*cut)
    return level


def bell_draw(rng, shape, scale, limit, cuts=(), kind=jnp.bfloat16):
    array = jax.random.normal(rng, shape, jnp.float32) * scale
    if len(cuts) > 0:
        array = levels(rng, shape, cuts, -0.22, 0.18) * array
    return jnp.clip(array, min=-limit, max=limit).astype(kind)


def setup_inputs(seed: int = 0) -> dict:
    keys = jax.random.split(jax.random.key(seed), 5)
    return {
        "sample": bell_draw(keys[0], (CIN, DIN, HIN, WIN), 1.0, 6.0, ((0, 8), (1, 64))),
        "first_weight": bell_draw(keys[1], (CMID, 27 * CIN), (27 * CIN) ** -0.5, 0.109375, ((0, 8),)),
        "second_weight": bell_draw(keys[2], (CMID, 27 * CMID), (27 * CMID) ** -0.5, 0.078125, ((0, 8),)),
        "cotangent": bell_draw(keys[3], (CMID, DOUT, HO, WO), 0.004, 0.023925781, ((0, 8), (1, 64))),
    }


LEAK = 0.3


def convolve(inputs, kernel, stride, depth_pad):
    return lax.conv_general_dilated(inputs[None], kernel, (stride, stride, stride), ((depth_pad, depth_pad), (1, 1), (1, 1)), dimension_numbers=("NCDHW", "OIDHW", "NCDHW"), preferred_element_type=jnp.float32)[0]


def as_kernel(weight, channels):
    return weight.reshape(weight.shape[0], 3, 3, 3, channels).transpose(0, 4, 1, 2, 3)


def tap_grads(grad_rows, padded, stride, depth_len, height, width):
    pieces = []
    for kd in range(3):
        for kh in range(3):
            for kw in range(3):
                piece = padded[:, kd:kd + stride * depth_len:stride, kh:kh + stride * height:stride, kw:kw + stride * width:stride]
                flat = piece.reshape(piece.shape[0], -1)
                pieces.append(jnp.dot(grad_rows, flat.T, preferred_element_type=jnp.float32))
    stacked = jnp.stack(pieces, axis=1)
    return stacked.reshape(stacked.shape[0], -1)


def reference(sample, first_weight, second_weight, cotangent):
    first_kernel = as_kernel(first_weight, CIN)
    second_kernel = as_kernel(second_weight, CMID)
    first_pre = convolve(sample, first_kernel, 2, 1)
    slope = jnp.where(first_pre > 0, 1.0, LEAK)
    first_act = (first_pre * slope).astype(jnp.bfloat16)
    second_out = convolve(first_act, second_kernel, 1, 1).astype(jnp.bfloat16)
    flipped = second_kernel.transpose(1, 0, 2, 3, 4)[:, :, ::-1, ::-1, ::-1]
    act_grad = convolve(cotangent, flipped, 1, 1)
    pre_grad = (act_grad * slope).astype(jnp.bfloat16)
    act_pad = jnp.pad(first_act, ((0, 0), (1, 1), (1, 1), (1, 1)))
    second_grad = tap_grads(cotangent.reshape(CMID, -1), act_pad, 1, DOUT, HO, WO)
    sample_pad = jnp.pad(sample, ((0, 0), (1, 1), (1, 1), (1, 1)))
    first_grad = tap_grads(pre_grad.reshape(CMID, -1), sample_pad, 2, DOUT, HO, WO)
    return second_out, first_grad, second_grad
```

```python
import jax
import jax.numpy as jnp
from jax import lax
from jax.experimental import pallas as pl
from jax.experimental.pallas import tpu as pltpu
from jax.sharding import PartitionSpec as P

LEAK = 0.3
F32 = jnp.float32
BF16 = jnp.bfloat16
MESH = pl.DeviceIdType.MESH

NZ, NY, NK, NX = 8, 4, 2, 4
DEPTH = NZ * NY * NK

S_SAMPLE = 0
S_ACT = 14
S_COT = 28
S_AGX = 30
S_AGZ = 33
S_B1 = 34
S_PG = 35
S_Y = 36
S_CORE = 38
S_YS = 39
S_ZS = 42
N_SEM = 49


def dot(a, b):
    return lax.dot_general(a, b, (((1,), (0,)), ((), ())), preferred_element_type=F32)


def dot_t(a, b):
    return lax.dot_general(a, b, (((1,), (1,)), ((), ())), preferred_element_type=F32)


def shift_matrix(rows, base):
    r = lax.broadcasted_iota(jnp.int32, (rows, 384), 0)
    c = lax.broadcasted_iota(jnp.int32, (rows, 384), 1)
    kw = c >> 7
    m = c & 127
    w = (m & 63) + kw - 1
    hit = (r == m + base + kw - 1) & (w >= 0) & (w < 64)
    return jnp.where(hit, 1.0, 0.0).astype(BF16)


def stride_matrix():
    r = lax.broadcasted_iota(jnp.int32, (256, 384), 0)
    c = lax.broadcasted_iota(jnp.int32, (256, 384), 1)
    kw = c >> 7
    i = (c >> 6) & 1
    w = 2 * (c & 63) + kw - 1
    hit = (r == i * 128 + w) & (w >= 0)
    return jnp.where(hit, 1.0, 0.0).astype(BF16)


def kernel(
    samp, w1, w2, cot,
    so, fgo, sgo,
    g, s, c3, ci, wv, ag32, agb, agr, az32, azb, azr, w1s, b1s, b1r, slope, act, pg2, x9, w2s, ys, yr,
    rsg, rfg, t, cr, u, yrs, v, zr, send_sems, recv_sems,
):
    d = lax.axis_index("depth")
    c = lax.axis_index("chan")
    core = lax.rem(d, 2)
    y = lax.rem(d // 2, NY)
    zl = d // (2 * NY)
    x = c // 2
    zh = lax.rem(c, 2)
    first = d == 0
    last = d == DEPTH - 1

    def chan_at(dx, flip=False):
        return lax.rem(x + dx + NX, NX) * 2 + (1 - zh if flip else zh)

    xdev = [(d, chan_at(k)) for k in (1, 2, 3)]
    zdev = (d, chan_at(0, True))
    kdev = (d + 1 - 2 * core, c)
    ydev = [(zl * 8 + lax.rem(y + k, NY) * 2 + core, c) for k in (1, 2, 3)]
    zldev = [(lax.rem(zl + k, NZ) * 8 + y * 2 + core, c) for k in range(1, 8)]
    up = (lax.rem(d + 1, DEPTH), c)
    down = (lax.rem(d + DEPTH - 1, DEPTH), c)
    right, left = xdev[0], xdev[2]

    pending = []

    def desc(k, src, dst, dev):
        return pltpu.make_async_remote_copy(
            src_ref=src, dst_ref=dst, send_sem=send_sems.at[k], recv_sem=recv_sems.at[k], device_id=dev, device_id_type=MESH
        )

    def send(k, src, dst, dev, cond=None):
        copy = desc(k, src, dst, dev)
        if cond is None:
            copy.start()
        else:
            pl.when(cond)(copy.start)
        pending.append((copy, cond))

    def recv(k, dst, dev, cond=None):
        copy = desc(k, dst, dst, dev)
        if cond is None:
            copy.wait_recv()
        else:
            pl.when(cond)(copy.wait_recv)

    c3[...] = jnp.zeros(c3.shape, BF16)
    act[:, 0:128] = jnp.zeros((256, 128), BF16)
    act[:, 640:768] = jnp.zeros((256, 128), BF16)
    g[32] = jnp.zeros((128, 128), BF16)

    @pl.when(first)
    def _():
        b1r[...] = jnp.zeros(b1r.shape, F32)
        yr[0] = jnp.zeros((32, 512), BF16)

    @pl.when(last)
    def _():
        pg2[32:64] = jnp.zeros((32, 512), BF16)
        yr[1] = jnp.zeros((32, 512), BF16)

    barrier = pltpu.get_barrier_semaphore()
    partners = xdev + [zdev, kdev] + ydev + zldev + [up, down]
    for dev in partners:
        pl.semaphore_signal(barrier, inc=1, device_id=dev, device_id_type=MESH)
    pl.semaphore_wait(barrier, len(partners))

    class Gather:
        def __init__(self, base, own, block):
            self.base, self.own, self.block = base, own, block

        def start(self):
            for i in range(2):
                send(self.base + i, self.own(i), self.block(c, i), zdev)
            for i in range(2):
                send(self.base + 2 + i, self.own(i), self.block(c, i), right)
                send(self.base + 4 + 1 - i, self.own(1 - i), self.block(c, 1 - i), left)

        def relay_x(self):
            b, blk = self.base, self.block
            from_left = blk(chan_at(-1), 0)
            recv(b + 2, from_left, left)
            send(b + 6, from_left, from_left, right)
            from_right = blk(chan_at(1), 1)
            recv(b + 5, from_right, right)
            send(b + 7, from_right, from_right, left)

        def relay_z(self, i):
            b, blk = self.base, self.block
            over = blk(chan_at(0, True), i)
            recv(b + i, over, zdev)
            send(b + 8 + i, over, over, right)
            send(b + 10 + i, over, over, left)

        def relay_zx(self):
            b, blk = self.base, self.block
            from_left = blk(chan_at(-1, True), 0)
            recv(b + 8, from_left, left)
            send(b + 12, from_left, from_left, right)
            from_right = blk(chan_at(1, True), 1)
            recv(b + 11, from_right, right)
            send(b + 13, from_right, from_right, left)

        def finish(self):
            b, blk = self.base, self.block
            recv(b + 3, blk(chan_at(-1), 1), left)
            recv(b + 4, blk(chan_at(1), 0), right)
            recv(b + 6, blk(chan_at(2), 0), left)
            recv(b + 7, blk(chan_at(2), 1), right)
            recv(b + 9, blk(chan_at(-1, True), 1), left)
            recv(b + 10, blk(chan_at(1, True), 0), right)
            recv(b + 12, blk(chan_at(2, True), 0), left)
            recv(b + 13, blk(chan_at(2, True), 1), right)

    sample_gather = Gather(
        S_SAMPLE,
        lambda i: samp.at[16 * i : 16 * i + 16],
        lambda r, i: g.at[16 * i : 16 * i + 16, pl.ds(pl.multiple_of(r * 16, 16), 16), :],
    )
    act_gather = Gather(
        S_ACT,
        lambda i: act.at[pl.ds(pl.multiple_of(c * 32 + 16 * i, 16), 16), 128:640],
        lambda r, i: act.at[pl.ds(pl.multiple_of(r * 32 + 16 * i, 16), 16), 128:640],
    )

    send(S_COT, cot, c3.at[64:96, 128:640], up, jnp.logical_not(last))
    send(S_COT + 1, cot, c3.at[0:32, 128:640], down, jnp.logical_not(first))
    sample_gather.start()

    c3[32:64, 128:640] = cot[...]
    g[0:32, pl.ds(pl.multiple_of(c * 16, 16), 16), :] = samp[...]
    for k in range(27):
        wv[32 * k : 32 * k + 32] = w2[:, 256 * k : 256 * k + 256]
    for k in range(3):
        w2s[32 * k : 32 * k + 32] = w2[:, 2304 * k : 2304 * k + 2304]
    w1s[0:32] = w1[:, 2304:3456]
    w1s[32:64] = w1[:, 0:1152]
    sh_two = shift_matrix(256, 64)
    sh_one = shift_matrix(128, 0)
    recv(S_COT, c3.at[64:96, 128:640], down, jnp.logical_not(first))
    recv(S_COT + 1, c3.at[0:32, 128:640], up, jnp.logical_not(last))

    def shifted(ref, j, kh):
        if kh == 1:
            return dot(ref[:, 128 * (j + 1) : 128 * (j + 2)], sh_one).astype(BF16)
        at = 128 * j if kh == 0 else 128 * (j + 1)
        return dot(ref[:, at : at + 256], sh_two).astype(BF16)

    for j in range(4):
        for kh in range(3):
            tile = shifted(c3, j, kh)
            for kw in range(3):
                for kd in range(3):
                    tap = 9 * kd + 3 * (2 - kh) + 2 - kw
                    ci[32 * tap : 32 * tap + 32, 128 * j : 128 * j + 128] = tile[32 * kd : 32 * kd + 32, 128 * kw : 128 * kw + 128]
    part = lax.dot_general(wv[...], ci[...], (((0,), (0,)), ((), ())), preferred_element_type=F32)
    ag32[...] = part
    agb[...] = part.astype(BF16)

    sample_gather.relay_x()
    for k in range(3):
        to = lax.rem(x + k + 1, NX)
        send(S_AGX + k, agb.at[pl.ds(pl.multiple_of(to * 64, 64), 64)], agr.at[k], xdev[k])
    sample_gather.relay_z(0)
    total = ag32[pl.ds(pl.multiple_of(x * 64, 64), 64)]
    for k in range(3):
        recv(S_AGX + k, agr.at[k], xdev[2 - k])
        total = total + agr[k].astype(F32)
    az32[...] = total
    azb[...] = total.astype(BF16)
    send(S_AGZ, azb.at[pl.ds(pl.multiple_of((1 - zh) * 32, 32), 32)], azr, zdev)
    sample_gather.relay_z(1)
    sample_gather.relay_zx()
    sample_gather.finish()

    stride = stride_matrix()
    for plane in (1, 0):
        for j in range(4):
            for kh in range(3):
                at = 4 * j + kh - 1
                low = g[16 * plane + at] if at >= 0 else g[32]
                tile = dot(jnp.concatenate([low, g[16 * plane + at + 2]], axis=1), stride).astype(BF16)
                for kw in range(3):
                    row = 128 * (3 * kh + kw)
                    s[plane, row : row + 128, 128 * j : 128 * j + 128] = tile[:, 128 * kw : 128 * kw + 128]
        if plane == 1:
            both = dot(w1s[...], s[1])
            b1s[...] = both[32:64]
            send(S_B1, b1s, b1r, up, jnp.logical_not(last))
    pre = both[0:32] + dot(w1[:, 1152:2304], s[0])
    recv(S_B1, b1r, down, jnp.logical_not(first))
    pre = pre + b1r[...]
    sl = jnp.where(pre > 0, 1.0, LEAK)
    act[pl.ds(pl.multiple_of(c * 32, 32), 32), 128:640] = (pre * sl).astype(BF16)
    act_gather.start()

    recv(S_AGZ, azr, zdev)
    grad = az32[pl.ds(pl.multiple_of(zh * 32, 32), 32)] + azr[...].astype(F32)
    pg2[0:32] = (grad * sl).astype(BF16)
    send(S_PG, pg2.at[0:32], pg2.at[32:64], down, jnp.logical_not(first))
    act_gather.relay_x()
    rfg[:, 1152:2304] = dot_t(pg2[0:32], s[0])
    rfg[:, 3456:3584] = jnp.zeros((32, 128), F32)
    recv(S_PG, pg2.at[32:64], up, jnp.logical_not(last))
    act_gather.relay_z(0)
    act_gather.relay_z(1)
    both = dot_t(pg2[...], s[1])
    rfg[:, 2304:3456] = both[0:32]
    rfg[:, 0:1152] = both[32:64]
    act_gather.relay_zx()
    act_gather.finish()

    for j in range(4):
        for kh in range(3):
            tile = shifted(act, j, kh)
            for kw in range(3):
                row = 256 * (3 * kh + kw)
                x9[row : row + 256, 128 * j : 128 * j + 128] = tile[:, 128 * kw : 128 * kw + 128]
    out = dot(w2s[...], x9[...])
    ys[0:32] = out[0:32].astype(BF16)
    ys[32:64] = out[64:96].astype(BF16)
    send(S_Y, ys.at[0:32], yr.at[0], up, jnp.logical_not(last))
    send(S_Y + 1, ys.at[32:64], yr.at[1], down, jnp.logical_not(first))
    grads = dot_t(c3[:, 128:640], x9[...])
    rsg[0:32, 0:2304] = grads[0:32]
    rsg[0:32, 2304:3456] = grads[32:64, 0:1152]
    rsg[32:64, 0:1152] = grads[32:64, 1152:2304]
    rsg[32:64, 1152:3456] = grads[64:96]
    rsg[:, 3456:3584] = jnp.zeros((64, 128), F32)

    for k in range(32):
        zz, yy, kk = k // 8, (k % 8) // 2, k % 2
        piece = rsg[:, 108 * k : 108 * k + 128].astype(BF16)
        t[kk, yy, zz] = piece[0:32]
        t[kk, yy, zz + 4] = piece[32:64]
        low = rfg[:, 54 * k : 54 * k + 64]
        high = rfg[:, 54 * (k + 32) : 54 * (k + 32) + 64]
        t[kk, yy, 8 + zz] = jnp.concatenate([low, high], axis=1).astype(BF16)
    send(S_CORE, t.at[1 - core], cr, kdev)
    recv(S_Y, yr.at[0], down, jnp.logical_not(first))
    recv(S_Y + 1, yr.at[1], up, jnp.logical_not(last))
    so[...] = (out[32:64] + yr[0].astype(F32) + yr[1].astype(F32)).astype(BF16)
    recv(S_CORE, cr, kdev)
    u[...] = (t[core].astype(F32) + cr[...].astype(F32)).astype(BF16)
    for k in range(3):
        send(S_YS + k, u.at[lax.rem(y + k + 1, NY)], yrs.at[k], ydev[k])
    total = u[y].astype(F32)
    for k in range(3):
        recv(S_YS + k, yrs.at[k], ydev[2 - k])
        total = total + yrs[k].astype(F32)
    total = total.astype(BF16)
    for k in range(8):
        v[k, 0] = total[k]
        v[k, 1] = total[8 + k % 4]
    for k in range(7):
        send(S_ZS + k, v.at[lax.rem(zl + k + 1, NZ)], zr.at[k], zldev[k])
    total = v[zl].astype(F32)
    for k in range(7):
        recv(S_ZS + k, zr.at[k], zldev[6 - k])
        total = total + zr[k].astype(F32)
    sgo[...] = total[0, :, 0:108]
    fgo[...] = jnp.where(zl < 4, total[1, :, 0:54], total[1, :, 64:118])

    for copy, cond in pending:
        if cond is None:
            copy.wait_send()
        else:
            pl.when(cond)(copy.wait_send)


def shards(sample, first_weight, second_weight, cotangent):
    samp = sample.transpose(1, 2, 0, 3).reshape(32, 16, 128)
    vmem = pl.BlockSpec(memory_space=pltpu.VMEM)
    so, fgo, sgo = pl.pallas_call(
        kernel,
        out_shape=(
            jax.ShapeDtypeStruct((32, 512), BF16),
            jax.ShapeDtypeStruct((32, 54), F32),
            jax.ShapeDtypeStruct((32, 108), F32),
        ),
        in_specs=[vmem] * 4,
        out_specs=(vmem, vmem, vmem),
        scratch_shapes=[
            pltpu.VMEM((33, 128, 128), BF16),
            pltpu.VMEM((2, 1152, 512), BF16),
            pltpu.VMEM((96, 768), BF16),
            pltpu.VMEM((864, 512), BF16),
            pltpu.VMEM((864, 256), BF16),
            pltpu.VMEM((256, 512), F32),
            pltpu.VMEM((256, 512), BF16),
            pltpu.VMEM((3, 64, 512), BF16),
            pltpu.VMEM((64, 512), F32),
            pltpu.VMEM((64, 512), BF16),
            pltpu.VMEM((32, 512), BF16),
            pltpu.VMEM((64, 1152), BF16),
            pltpu.VMEM((32, 512), F32),
            pltpu.VMEM((32, 512), F32),
            pltpu.VMEM((32, 512), F32),
            pltpu.VMEM((256, 768), BF16),
            pltpu.VMEM((64, 512), BF16),
            pltpu.VMEM((2304, 512), BF16),
            pltpu.VMEM((96, 2304), BF16),
            pltpu.VMEM((64, 512), BF16),
            pltpu.VMEM((2, 32, 512), BF16),
            pltpu.VMEM((64, 3584), F32),
            pltpu.VMEM((32, 3584), F32),
            pltpu.VMEM((2, 4, 12, 32, 128), BF16),
            pltpu.VMEM((4, 12, 32, 128), BF16),
            pltpu.VMEM((4, 12, 32, 128), BF16),
            pltpu.VMEM((3, 12, 32, 128), BF16),
            pltpu.VMEM((8, 2, 32, 128), BF16),
            pltpu.VMEM((7, 2, 32, 128), BF16),
            pltpu.SemaphoreType.DMA((N_SEM,)),
            pltpu.SemaphoreType.DMA((N_SEM,)),
        ],
        compiler_params=pltpu.CompilerParams(collective_id=0, has_side_effects=True, vmem_limit_bytes=40 * 1024 * 1024),
        name="slab_pair",
    )(samp, first_weight, second_weight, cotangent.reshape(32, 512))
    return so.reshape(32, 1, 8, 64), fgo, sgo


def solution(mesh):
    return jax.shard_map(
        shards,
        mesh=mesh,
        in_specs=(
            P("chan", "depth", None, None),
            P("chan", None),
            P("chan", None),
            P("chan", "depth", None, None),
        ),
        out_specs=(P("chan", "depth", None, None), P("chan", "depth"), P("chan", "depth")),
        check_vma=False,
    )
```

```python
import jax
import jax.numpy as jnp
from jax import lax
from jax.experimental import pallas as pl
from jax.experimental.pallas import tpu as pltpu
from jax.sharding import PartitionSpec as P

LEAK = 0.3
F32 = jnp.float32
BF16 = jnp.bfloat16
MESH = pl.DeviceIdType.MESH

NZ, NY, NK, NX = 8, 4, 2, 4
DEPTH = NZ * NY * NK

S_Z = 0
S_OX = 3
S_FX = 9
S_ACT = 18
S_COT = 21
S_AGX = 23
S_AGZ = 26
S_B1 = 27
S_PG = 28
S_Y = 29
S_KF = 31
S_KS = 32
S_YF = 33
S_YS = 36
S_ZF = 39
S_ZS = 46
S_WZ = 53
S_WL = 54
S_WY = 61
S_WK = 64
N_SEM = 65

CHUNKS = ((16, 32), (7, 16), (0, 7))


def dot(a, b):
    return lax.dot_general(a, b, (((1,), (0,)), ((), ())), preferred_element_type=F32)


def dot_t(a, b):
    return lax.dot_general(a, b, (((1,), (1,)), ((), ())), preferred_element_type=F32)


def shift_matrix(rows, base):
    r = lax.broadcasted_iota(jnp.int32, (rows, 384), 0)
    c = lax.broadcasted_iota(jnp.int32, (rows, 384), 1)
    kw = c >> 7
    m = c & 127
    w = (m & 63) + kw - 1
    hit = (r == m + base + kw - 1) & (w >= 0) & (w < 64)
    return jnp.where(hit, 1.0, 0.0).astype(BF16)


def stride_matrix():
    r = lax.broadcasted_iota(jnp.int32, (256, 384), 0)
    c = lax.broadcasted_iota(jnp.int32, (256, 384), 1)
    kw = c >> 7
    i = (c >> 6) & 1
    w = 2 * (c & 63) + kw - 1
    hit = (r == i * 128 + w) & (w >= 0)
    return jnp.where(hit, 1.0, 0.0).astype(BF16)


def swap_matrix(rows, fast):
    slow = rows // fast
    bits = slow.bit_length() - 1
    r = lax.broadcasted_iota(jnp.int32, (rows, rows), 0)
    k = lax.broadcasted_iota(jnp.int32, (rows, rows), 1)
    hit = ((k >> bits) == (r & (fast - 1))) & ((k & (slow - 1)) == (r >> (fast.bit_length() - 1)))
    return jnp.where(hit, 1.0, 0.0).astype(BF16)


def kernel(
    samp_hbm, w1_hbm, w2_hbm, cot_hbm,
    so, fgo, sgo,
    sraw, w1, w2, craw, own, cot, g, s, c3, ci, wv, ag32, agb, agr, az32, azb, azr, wo, wp, w1p, w1m, b1s, b1r,
    slope, act, pg2, x9, w2s, ys, yr, rsg, rfg, tf, cf, uf, yf, vf, zf, ts, cs, us, yg, vs, zs,
    send_sems, recv_sems, load_sems,
):
    d = lax.axis_index("depth")
    c = lax.axis_index("chan")
    core = lax.rem(d, 2)
    y = lax.rem(d // 2, NY)
    zl = d // (2 * NY)
    x = c // 2
    zh = lax.rem(c, 2)
    first = d == 0
    last = d == DEPTH - 1

    def chan_at(dx, flip=False):
        return lax.rem(x + dx + NX, NX) * 2 + (1 - zh if flip else zh)

    xdev = [(d, chan_at(k)) for k in (1, 2, 3)]
    zdev = (d, chan_at(0, True))
    kdev = (d + 1 - 2 * core, c)
    ydev = [(zl * 8 + lax.rem(y + k, NY) * 2 + core, c) for k in (1, 2, 3)]
    zldev = [(lax.rem(zl + k, NZ) * 8 + y * 2 + core, c) for k in range(1, 8)]
    up = (lax.rem(d + 1, DEPTH), c)
    down = (lax.rem(d + DEPTH - 1, DEPTH), c)

    barrier = pltpu.get_barrier_semaphore()
    partners = [zdev] + zldev + xdev + ydev + [kdev, up, down]
    for dev in partners:
        pl.semaphore_signal(barrier, inc=1, device_id=dev, device_id_type=MESH)
    loads = [
        pltpu.make_async_copy(src, dst, load_sems.at[i])
        for i, (src, dst) in enumerate(((samp_hbm, sraw), (cot_hbm, craw), (w1_hbm, w1), (w2_hbm, w2)))
    ]
    for load in loads:
        load.start()

    pending = []

    def desc(k, src, dst, dev):
        return pltpu.make_async_remote_copy(
            src_ref=src, dst_ref=dst, send_sem=send_sems.at[k], recv_sem=recv_sems.at[k], device_id=dev, device_id_type=MESH
        )

    def send(k, src, dst, dev, cond=None):
        copy = desc(k, src, dst, dev)
        if cond is None:
            copy.start()
        else:
            pl.when(cond)(copy.start)
        pending.append((copy, cond))

    def recv(k, dst, dev, cond=None):
        copy = desc(k, dst, dst, dev)
        if cond is None:
            copy.wait_recv()
        else:
            pl.when(cond)(copy.wait_recv)

    def rows(start, size):
        return pl.ds(pl.multiple_of(start, size), size)

    def sample_block(r, lines):
        return g.at[lines[0] : lines[1], rows(r * 16, 16), :]

    loads[0].wait()
    swap = swap_matrix(256, 16)
    for plane in range(2):
        lines = dot(swap, sraw[:, plane].reshape(256, 128))
        own[16 * plane : 16 * plane + 16] = lines.astype(BF16).reshape(16, 16, 128)
    loads[1].wait()
    lines = dot(swap_matrix(256, 32), craw[:, 0].astype(F32).reshape(256, 64).astype(BF16))
    for j in range(4):
        pair = jnp.concatenate([lines[64 * j : 64 * j + 32], lines[64 * j + 32 : 64 * j + 64]], axis=1)
        cot[:, 128 * j : 128 * j + 128] = pair.astype(BF16)
    loads[2].wait()
    wo[...] = jnp.zeros(wo.shape, BF16)
    for k in range(27):
        wo[k // 4, k % 4] = w1[:, 128 * k : 128 * k + 128].reshape(2, 16, 128)
    pl.semaphore_wait(barrier, len(partners))

    send(S_WZ, wo.at[zl, y, core], wp.at[zl, y, core], zdev)
    for i, lines in enumerate(CHUNKS):
        send(S_Z + i, own.at[lines[0] : lines[1]], sample_block(c, lines), zdev)
    send(S_COT, cot, c3.at[64:96, 128:640], up, jnp.logical_not(last))
    send(S_COT + 1, cot, c3.at[0:32, 128:640], down, jnp.logical_not(first))
    for i, lines in enumerate(((16, 32), (0, 16))):
        for k in range(3):
            send(S_OX + 3 * i + k, own.at[lines[0] : lines[1]], sample_block(c, lines), xdev[k])

    c3[:, 0:128] = jnp.zeros((96, 128), BF16)
    c3[:, 640:768] = jnp.zeros((96, 128), BF16)
    act[:, 0:128] = jnp.zeros((256, 128), BF16)
    act[:, 640:768] = jnp.zeros((256, 128), BF16)
    g[32] = jnp.zeros((128, 128), BF16)

    @pl.when(first)
    def _():
        c3[64:96, 128:640] = jnp.zeros((32, 512), BF16)

    @pl.when(last)
    def _():
        c3[0:32, 128:640] = jnp.zeros((32, 512), BF16)
        pg2[32:64] = jnp.zeros((32, 512), BF16)

    c3[32:64, 128:640] = cot[...]
    g[0:32, rows(c * 16, 16), :] = own[...]
    loads[3].wait()
    for k in range(27):
        wv[32 * k : 32 * k + 32] = w2[:, 256 * k : 256 * k + 256]
    for k in range(3):
        w2s[32 * k : 32 * k + 32] = w2[:, 2304 * k : 2304 * k + 2304]
    mine = pl.multiple_of(zh * 32, 32)
    theirs = pl.multiple_of((1 - zh) * 32, 32)
    w1p[pl.ds(mine, 32)] = w1[:, 2304:3456]
    w1p[pl.ds(mine + 64, 32)] = w1[:, 0:1152]
    w1m[pl.ds(mine, 32)] = w1[:, 1152:2304]
    sh_two = shift_matrix(256, 64)
    sh_one = shift_matrix(128, 0)
    recv(S_COT, c3.at[64:96, 128:640], down, jnp.logical_not(first))
    recv(S_COT + 1, c3.at[0:32, 128:640], up, jnp.logical_not(last))

    def shifted(ref, j, kh):
        if kh == 1:
            return dot(ref[:, 128 * (j + 1) : 128 * (j + 2)], sh_one).astype(BF16)
        at = 128 * j if kh == 0 else 128 * (j + 1)
        return dot(ref[:, at : at + 256], sh_two).astype(BF16)

    for j in range(4):
        for kh in range(3):
            tile = shifted(c3, j, kh)
            for kw in range(3):
                for kd in range(3):
                    tap = 9 * kd + 3 * (2 - kh) + 2 - kw
                    ci[32 * tap : 32 * tap + 32, 128 * j : 128 * j + 128] = tile[32 * kd : 32 * kd + 32, 128 * kw : 128 * kw + 128]
    part = lax.dot_general(wv[...], ci[...], (((0,), (0,)), ((), ())), preferred_element_type=F32)
    ag32[...] = part
    agb[...] = part.astype(BF16)
    for k in range(3):
        send(S_AGX + k, agb.at[rows(lax.rem(x + k + 1, NX) * 64, 64)], agr.at[k], xdev[k])

    recv(S_WZ, wp.at[zl, y, core], zdev)
    for k in range(7):
        send(S_WL + k, wp.at[zl, y, core], wp.at[zl, y, core], zldev[k])

    total = ag32[rows(x * 64, 64)]
    for k in range(3):
        recv(S_AGX + k, agr.at[k], xdev[2 - k])
        total = total + agr[k].astype(F32)
    az32[...] = total
    azb[...] = total.astype(BF16)
    send(S_AGZ, azb.at[pl.ds(theirs, 32)], azr, zdev)

    def across(i):
        block = sample_block(chan_at(0, True), CHUNKS[i])
        recv(S_Z + i, block, zdev)
        for k in range(3):
            send(S_FX + 3 * i + k, block, block, xdev[k])

    def arrived(i):
        for k in range(3):
            recv(S_FX + 3 * i + k, sample_block(chan_at(3 - k, True), CHUNKS[i]), xdev[2 - k])

    across(0)
    for k in range(7):
        recv(S_WL + k, wp.at[lax.rem(zl + 7 - k, NZ), y, core], zldev[6 - k])
    for k in range(3):
        send(S_WY + k, wp.at[:, y, core], wp.at[:, y, core], ydev[k])
    across(1)
    across(2)
    for i, lines in enumerate(((16, 32), (0, 16))):
        for k in range(3):
            recv(S_OX + 3 * i + k, sample_block(chan_at(3 - k), lines), xdev[2 - k])
    for k in range(3):
        recv(S_WY + k, wp.at[:, lax.rem(y + 3 - k, NY), core], ydev[2 - k])
    send(S_WK, wp.at[:, :, core], wp.at[:, :, core], kdev)
    stride = stride_matrix()

    def strided(plane, j):
        for kh in range(3):
            at = 4 * j + kh - 1
            low = g[16 * plane + at] if at >= 0 else g[32]
            tile = dot(jnp.concatenate([low, g[16 * plane + at + 2]], axis=1), stride).astype(BF16)
            for kw in range(3):
                row = 128 * (3 * kh + kw)
                s[plane, row : row + 128, 128 * j : 128 * j + 128] = tile[:, 128 * kw : 128 * kw + 128]

    arrived(0)
    for j in range(4):
        strided(1, j)
    recv(S_WK, wp.at[:, :, 1 - core], kdev)
    for k in range(27):
        tile = wp[k // 4, k % 4].reshape(32, 128)
        at = 128 * (k % 9)
        if k // 9 == 1:
            w1m[pl.ds(theirs, 32), at : at + 128] = tile
        else:
            w1p[pl.ds(theirs + (64 if k < 9 else 0), 32), at : at + 128] = tile
    both = dot(w1p[...], s[1])
    b1s[...] = both[64:128]
    send(S_B1, b1s, b1r, up, jnp.logical_not(last))
    arrived(1)
    halves = [None, None]
    for half in (1, 0):
        if half == 0:
            arrived(2)
        strided(0, 2 * half)
        strided(0, 2 * half + 1)
        halves[half] = dot(w1m[...], s[0, :, 256 * half : 256 * half + 256])
    pre = both[0:64] + jnp.concatenate(halves, axis=1)
    recv(S_B1, b1r, down, jnp.logical_not(first))
    pre = pre + jnp.where(first, 0.0, b1r[...])
    sl = jnp.where(pre > 0, 1.0, LEAK)
    group = act.at[rows(x * 64, 64), 128:640]
    group[...] = (pre * sl).astype(BF16)
    for k in range(3):
        send(S_ACT + k, group, group, xdev[k])
    slope[...] = sl

    recv(S_AGZ, azr, zdev)
    grad = az32[pl.ds(mine, 32)] + azr[...].astype(F32)
    pg2[0:32] = (grad * slope[pl.ds(mine, 32)]).astype(BF16)
    send(S_PG, pg2.at[0:32], pg2.at[32:64], down, jnp.logical_not(first))
    rfg[:, 1152:2304] = dot_t(pg2[0:32], s[0])
    rfg[:, 3456:3584] = jnp.zeros((32, 128), F32)
    recv(S_PG, pg2.at[32:64], up, jnp.logical_not(last))
    both = dot_t(pg2[...], s[1])
    rfg[:, 2304:3456] = both[0:32]
    rfg[:, 0:1152] = both[32:64]

    for k in range(32):
        low = rfg[:, 54 * k : 54 * k + 64]
        high = rfg[:, 54 * (k + 32) : 54 * (k + 32) + 64]
        tf[k % 2, (k % 8) // 2, k // 8] = jnp.concatenate([low, high], axis=1).astype(BF16)
    send(S_KF, tf.at[1 - core], cf, kdev)

    for k in range(3):
        recv(S_ACT + k, act.at[rows(lax.rem(x + 3 - k, NX) * 64, 64), 128:640], xdev[2 - k])
    recv(S_KF, cf, kdev)
    uf[...] = (tf[core].astype(F32) + cf[...].astype(F32)).astype(BF16)
    for k in range(3):
        send(S_YF + k, uf.at[lax.rem(y + k + 1, NY)], yf.at[k], ydev[k])
    for j in range(4):
        for kh in range(3):
            tile = shifted(act, j, kh)
            for kw in range(3):
                row = 256 * (3 * kh + kw)
                x9[row : row + 256, 128 * j : 128 * j + 128] = tile[:, 128 * kw : 128 * kw + 128]
    grads = dot_t(c3[:, 128:640], x9[...])
    rsg[0:32, 0:2304] = grads[0:32]
    rsg[0:32, 2304:3456] = grads[32:64, 0:1152]
    rsg[32:64, 0:1152] = grads[32:64, 1152:2304]
    rsg[32:64, 1152:3456] = grads[64:96]
    rsg[:, 3456:3584] = jnp.zeros((64, 128), F32)
    for k in range(32):
        piece = rsg[:, 108 * k : 108 * k + 128].astype(BF16)
        ts[k % 2, (k % 8) // 2, k // 8] = piece[0:32]
        ts[k % 2, (k % 8) // 2, k // 8 + 4] = piece[32:64]
    send(S_KS, ts.at[1 - core], cs, kdev)

    total = uf[y].astype(F32)
    for k in range(3):
        recv(S_YF + k, yf.at[k], ydev[2 - k])
        total = total + yf[k].astype(F32)
    vf[...] = total.astype(BF16)
    for k in range(7):
        send(S_ZF + k, vf.at[lax.rem(zl + k + 1, 4)], zf.at[k], zldev[k])

    recv(S_KS, cs, kdev)
    us[...] = (ts[core].astype(F32) + cs[...].astype(F32)).astype(BF16)
    for k in range(3):
        send(S_YS + k, us.at[lax.rem(y + k + 1, NY)], yg.at[k], ydev[k])

    out = dot(w2s[...], x9[...])
    ys[0:32] = out[0:32].astype(BF16)
    ys[32:64] = out[64:96].astype(BF16)
    send(S_Y, ys.at[0:32], yr.at[0], up, jnp.logical_not(last))
    send(S_Y + 1, ys.at[32:64], yr.at[1], down, jnp.logical_not(first))

    total = us[y].astype(F32)
    for k in range(3):
        recv(S_YS + k, yg.at[k], ydev[2 - k])
        total = total + yg[k].astype(F32)
    vs[...] = total.astype(BF16)
    for k in range(7):
        send(S_ZS + k, vs.at[lax.rem(zl + k + 1, NZ)], zs.at[k], zldev[k])

    recv(S_Y, yr.at[0], down, jnp.logical_not(first))
    recv(S_Y + 1, yr.at[1], up, jnp.logical_not(last))
    before = jnp.where(first, 0.0, yr[0].astype(F32))
    after = jnp.where(last, 0.0, yr[1].astype(F32))
    so[...] = (out[32:64] + before + after).astype(BF16)

    total = vf[lax.rem(zl, 4)].astype(F32)
    for k in range(7):
        recv(S_ZF + k, zf.at[k], zldev[6 - k])
        total = total + zf[k].astype(F32)
    fgo[...] = jnp.where(zl < 4, total[:, 0:54], total[:, 64:118])
    total = vs[zl].astype(F32)
    for k in range(7):
        recv(S_ZS + k, zs.at[k], zldev[6 - k])
        total = total + zs[k].astype(F32)
    sgo[...] = total[:, 0:108]

    for copy, cond in pending:
        if cond is None:
            copy.wait_send()
        else:
            pl.when(cond)(copy.wait_send)


def shards(sample, first_weight, second_weight, cotangent):
    vmem = pl.BlockSpec(memory_space=pltpu.VMEM)
    hbm = pl.BlockSpec(memory_space=pltpu.HBM)
    b16 = [
        (16, 2, 16, 128), (32, 3456), (32, 6912), (32, 1, 8, 64), (32, 16, 128), (32, 512), (33, 128, 128),
        (2, 1152, 512), (96, 768), (864, 512), (864, 256),
    ]
    scratch = [pltpu.VMEM(shape, BF16) for shape in b16]
    scratch += [pltpu.VMEM((256, 512), F32)]
    scratch += [pltpu.VMEM((256, 512), BF16), pltpu.VMEM((3, 64, 512), BF16), pltpu.VMEM((64, 512), F32)]
    scratch += [pltpu.VMEM((64, 512), BF16), pltpu.VMEM((32, 512), BF16)]
    scratch += [pltpu.VMEM((8, 4, 2, 16, 128), BF16)] * 2
    scratch += [pltpu.VMEM((128, 1152), BF16), pltpu.VMEM((64, 1152), BF16)]
    scratch += [pltpu.VMEM((64, 512), F32)] * 3
    scratch += [pltpu.VMEM(shape, BF16) for shape in ((256, 768), (64, 512), (2304, 512), (96, 2304), (64, 512), (2, 32, 512))]
    scratch += [pltpu.VMEM((64, 3584), F32), pltpu.VMEM((32, 3584), F32)]
    for n in (4, 8):
        shapes = ((2, 4, n), (4, n), (4, n), (3, n), (n,), (7,))
        scratch += [pltpu.VMEM(shape + (32, 128), BF16) for shape in shapes]
    scratch += [pltpu.SemaphoreType.DMA((N_SEM,))] * 2 + [pltpu.SemaphoreType.DMA((4,))]
    so, fgo, sgo = pl.pallas_call(
        kernel,
        out_shape=(
            jax.ShapeDtypeStruct((32, 512), BF16),
            jax.ShapeDtypeStruct((32, 54), F32),
            jax.ShapeDtypeStruct((32, 108), F32),
        ),
        in_specs=[hbm] * 4,
        out_specs=(vmem, vmem, vmem),
        scratch_shapes=scratch,
        compiler_params=pltpu.CompilerParams(collective_id=0, has_side_effects=True, vmem_limit_bytes=48 * 1024 * 1024),
        name="slab_pair",
    )(sample, first_weight, second_weight, cotangent)
    return so.reshape(32, 1, 8, 64), fgo, sgo


def solution(mesh):
    return jax.shard_map(
        shards,
        mesh=mesh,
        in_specs=(
            P("chan", "depth", None, None),
            P("chan", None),
            P("chan", None),
            P("chan", "depth", None, None),
        ),
        out_specs=(P("chan", "depth", None, None), P("chan", "depth"), P("chan", "depth")),
        check_vma=False,
    )
```

```python
import jax
import jax.numpy as jnp
from jax import lax
from jax.experimental import pallas as pl
from jax.experimental.pallas import tpu as pltpu
from jax.sharding import PartitionSpec as P

LEAK = 0.3
F32 = jnp.float32
BF16 = jnp.bfloat16
MESH = pl.DeviceIdType.MESH

NZ, NY, NK, NX = 8, 4, 2, 4
DEPTH = NZ * NY * NK

S_Z = 0
S_OX = 3
S_FX = 9
S_ACT = 18
S_COT = 21
S_AGX = 23
S_AGZ = 26
S_B1 = 27
S_PG = 28
S_Y = 29
S_KF = 31
S_KS = 32
S_YF = 33
S_YS = 36
S_ZF = 39
S_ZS = 46
S_WZ = 53
S_WY = 54
S_WK = 57
N_SEM = 58

VMEM_BYTES = 64 * 1024 * 1024 - 16 * 1024

CHUNKS = ((16, 32), (7, 16), (0, 7))


def dot(a, b):
    return lax.dot_general(a, b, (((1,), (0,)), ((), ())), preferred_element_type=F32)


def dot_t(a, b):
    return lax.dot_general(a, b, (((1,), (1,)), ((), ())), preferred_element_type=F32)


def shift_matrix(rows, base):
    r = lax.broadcasted_iota(jnp.int32, (rows, 384), 0)
    c = lax.broadcasted_iota(jnp.int32, (rows, 384), 1)
    kw = c >> 7
    m = c & 127
    w = (m & 63) + kw - 1
    hit = (r == m + base + kw - 1) & (w >= 0) & (w < 64)
    return jnp.where(hit, 1.0, 0.0).astype(BF16)


def stride_matrix():
    r = lax.broadcasted_iota(jnp.int32, (256, 384), 0)
    c = lax.broadcasted_iota(jnp.int32, (256, 384), 1)
    kw = c >> 7
    i = (c >> 6) & 1
    w = 2 * (c & 63) + kw - 1
    hit = (r == i * 128 + w) & (w >= 0)
    return jnp.where(hit, 1.0, 0.0).astype(BF16)


def swap_matrix(rows, fast):
    slow = rows // fast
    bits = slow.bit_length() - 1
    r = lax.broadcasted_iota(jnp.int32, (rows, rows), 0)
    k = lax.broadcasted_iota(jnp.int32, (rows, rows), 1)
    hit = ((k >> bits) == (r & (fast - 1))) & ((k & (slow - 1)) == (r >> (fast.bit_length() - 1)))
    return jnp.where(hit, 1.0, 0.0).astype(BF16)


def kernel(
    samp_hbm, w1_hbm, w2_hbm, cot_hbm,
    so, fgo, sgo,
    sraw, w1, w2, craw, own, cot, g, s, c3, ci, wv, ag32, agb, agr, az32, azb, azr, wo, wp, w1p, w1m, b1s, b1r,
    slope, act, pg2, x9, w2s, ys, yr, rsg, rfg, tf, cf, uf, yf, vf, zf, ts, cs, us, yg, vs, zs,
    send_sems, recv_sems, load_sems,
):
    d = lax.axis_index("depth")
    c = lax.axis_index("chan")
    core = lax.rem(d, 2)
    y = lax.rem(d // 2, NY)
    zl = d // (2 * NY)
    x = c // 2
    zh = lax.rem(c, 2)
    first = d == 0
    last = d == DEPTH - 1

    def chan_at(dx, flip=False):
        return lax.rem(x + dx + NX, NX) * 2 + (1 - zh if flip else zh)

    xdev = [(d, chan_at(k)) for k in (1, 2, 3)]
    zdev = (d, chan_at(0, True))
    kdev = (d + 1 - 2 * core, c)
    ydev = [(zl * 8 + lax.rem(y + k, NY) * 2 + core, c) for k in (1, 2, 3)]
    zldev = [(lax.rem(zl + k, NZ) * 8 + y * 2 + core, c) for k in range(1, 8)]
    up = (lax.rem(d + 1, DEPTH), c)
    down = (lax.rem(d + DEPTH - 1, DEPTH), c)

    barrier = pltpu.get_barrier_semaphore()
    partners = [zdev] + zldev + xdev + ydev + [kdev, up, down]
    for dev in partners:
        pl.semaphore_signal(barrier, inc=1, device_id=dev, device_id_type=MESH)
    loads = [
        pltpu.make_async_copy(src, dst, load_sems.at[i])
        for i, (src, dst) in enumerate(((samp_hbm, sraw), (cot_hbm, craw), (w1_hbm, w1), (w2_hbm, w2)))
    ]
    for load in loads:
        load.start()

    pending = []

    def desc(k, src, dst, dev):
        return pltpu.make_async_remote_copy(
            src_ref=src, dst_ref=dst, send_sem=send_sems.at[k], recv_sem=recv_sems.at[k], device_id=dev, device_id_type=MESH
        )

    def send(k, src, dst, dev, cond=None):
        copy = desc(k, src, dst, dev)
        if cond is None:
            copy.start()
        else:
            pl.when(cond)(copy.start)
        pending.append((copy, cond))

    def recv(k, dst, dev, cond=None):
        copy = desc(k, dst, dst, dev)
        if cond is None:
            copy.wait_recv()
        else:
            pl.when(cond)(copy.wait_recv)

    def rows(start, size):
        return pl.ds(pl.multiple_of(start, size), size)

    def sample_block(r, lines):
        return g.at[lines[0] : lines[1], rows(r * 16, 16), :]

    loads[0].wait()
    swap = swap_matrix(256, 16)
    for plane in range(2):
        lines = dot(swap, sraw[:, plane].reshape(256, 128))
        own[16 * plane : 16 * plane + 16] = lines.astype(BF16).reshape(16, 16, 128)
    loads[1].wait()
    lines = dot(swap_matrix(256, 32), craw[:, 0].astype(F32).reshape(256, 64).astype(BF16))
    for j in range(4):
        pair = jnp.concatenate([lines[64 * j : 64 * j + 32], lines[64 * j + 32 : 64 * j + 64]], axis=1)
        cot[:, 128 * j : 128 * j + 128] = pair.astype(BF16)
    loads[2].wait()
    wo[3, 1] = jnp.zeros((7, 16, 128), BF16)
    for k in range(54):
        at = 16 * (k % 2)
        wo[k // 14, k // 7 % 2, k % 7] = w1[at : at + 16, 128 * (k // 2) : 128 * (k // 2) + 128]
    pl.semaphore_wait(barrier, len(partners))

    send(S_WZ, wo.at[y, core], wp.at[y, core], zdev)
    over = [desc(S_Z + i, own.at[a:b], sample_block(c, (a, b)), zdev) for i, (a, b) in enumerate(CHUNKS)]
    over[0].start()
    send(S_COT, cot, c3.at[64:96, 128:640], up, jnp.logical_not(last))
    send(S_COT + 1, cot, c3.at[0:32, 128:640], down, jnp.logical_not(first))
    for i, lines in enumerate(((16, 32), (0, 16))):
        for k in range(3):
            send(S_OX + 3 * i + k, own.at[lines[0] : lines[1]], sample_block(c, lines), xdev[k])

    c3[:, 0:128] = jnp.zeros((96, 128), BF16)
    c3[:, 640:768] = jnp.zeros((96, 128), BF16)
    act[:, 0:128] = jnp.zeros((256, 128), BF16)
    act[:, 640:768] = jnp.zeros((256, 128), BF16)
    g[32] = jnp.zeros((128, 128), BF16)

    @pl.when(first)
    def _():
        c3[64:96, 128:640] = jnp.zeros((32, 512), BF16)

    @pl.when(last)
    def _():
        c3[0:32, 128:640] = jnp.zeros((32, 512), BF16)
        pg2[32:64] = jnp.zeros((32, 512), BF16)

    c3[32:64, 128:640] = cot[...]
    g[0:32, rows(c * 16, 16), :] = own[...]
    loads[3].wait()
    for k in range(27):
        wv[32 * k : 32 * k + 32] = w2[:, 256 * k : 256 * k + 256]
    for k in range(3):
        w2s[32 * k : 32 * k + 32] = w2[:, 2304 * k : 2304 * k + 2304]
    mine = pl.multiple_of(zh * 32, 32)
    theirs = pl.multiple_of((1 - zh) * 32, 32)
    w1p[pl.ds(mine, 32)] = w1[:, 2304:3456]
    w1p[pl.ds(mine + 64, 32)] = w1[:, 0:1152]
    w1m[pl.ds(mine, 32)] = w1[:, 1152:2304]
    sh_two = shift_matrix(256, 64)
    sh_one = shift_matrix(128, 0)
    recv(S_COT, c3.at[64:96, 128:640], down, jnp.logical_not(first))
    recv(S_COT + 1, c3.at[0:32, 128:640], up, jnp.logical_not(last))

    def shifted(ref, j, kh):
        if kh == 1:
            return dot(ref[:, 128 * (j + 1) : 128 * (j + 2)], sh_one).astype(BF16)
        at = 128 * j if kh == 0 else 128 * (j + 1)
        return dot(ref[:, at : at + 256], sh_two).astype(BF16)

    for j in range(4):
        for kh in range(3):
            tile = shifted(c3, j, kh)
            for kw in range(3):
                for kd in range(3):
                    tap = 9 * kd + 3 * (2 - kh) + 2 - kw
                    ci[32 * tap : 32 * tap + 32, 128 * j : 128 * j + 128] = tile[32 * kd : 32 * kd + 32, 128 * kw : 128 * kw + 128]
    part = lax.dot_general(wv[...], ci[...], (((0,), (0,)), ((), ())), preferred_element_type=F32)
    ag32[...] = part
    agb[...] = part.astype(BF16)
    for k in range(3):
        send(S_AGX + k, agb.at[rows(lax.rem(x + k + 1, NX) * 64, 64)], agr.at[k], xdev[k])

    over[0].wait_send()
    over[1].start()
    recv(S_WZ, wp.at[y, core], zdev)
    for k in range(3):
        send(S_WY + k, wp.at[y, core], wp.at[y, core], ydev[k])

    over[1].wait_send()
    over[2].start()
    total = ag32[rows(x * 64, 64)]
    for k in range(3):
        recv(S_AGX + k, agr.at[k], xdev[2 - k])
        total = total + agr[k].astype(F32)
    az32[...] = total
    azb[...] = total.astype(BF16)
    over[2].wait_send()
    send(S_AGZ, azb.at[pl.ds(theirs, 32)], azr, zdev)

    def across(i):
        block = sample_block(chan_at(0, True), CHUNKS[i])
        recv(S_Z + i, block, zdev)
        for k in range(3):
            send(S_FX + 3 * i + k, block, block, xdev[k])

    def arrived(i):
        for k in range(3):
            recv(S_FX + 3 * i + k, sample_block(chan_at(3 - k, True), CHUNKS[i]), xdev[2 - k])

    across(0)
    for k in range(3):
        recv(S_WY + k, wp.at[lax.rem(y + 3 - k, NY), core], ydev[2 - k])
    send(S_WK, wp.at[:, core], wp.at[:, core], kdev)
    across(1)
    across(2)
    for i, lines in enumerate(((16, 32), (0, 16))):
        for k in range(3):
            recv(S_OX + 3 * i + k, sample_block(chan_at(3 - k), lines), xdev[2 - k])
    stride = stride_matrix()

    def strided(plane, j):
        for kh in range(3):
            at = 4 * j + kh - 1
            low = g[16 * plane + at] if at >= 0 else g[32]
            tile = dot(jnp.concatenate([low, g[16 * plane + at + 2]], axis=1), stride).astype(BF16)
            for kw in range(3):
                row = 128 * (3 * kh + kw)
                s[plane, row : row + 128, 128 * j : 128 * j + 128] = tile[:, 128 * kw : 128 * kw + 128]

    arrived(0)
    for j in range(4):
        strided(1, j)
    recv(S_WK, wp.at[:, 1 - core], kdev)
    for k in range(54):
        tile = wp[k // 14, k // 7 % 2, k % 7]
        at = 128 * (k // 2 % 9)
        row = theirs + 16 * (k % 2)
        if k // 18 == 1:
            w1m[pl.ds(row, 16), at : at + 128] = tile
        else:
            w1p[pl.ds(row + (64 if k < 18 else 0), 16), at : at + 128] = tile
    both = dot(w1p[...], s[1])
    b1s[...] = both[64:128]
    send(S_B1, b1s, b1r, up, jnp.logical_not(last))
    arrived(1)
    halves = [None, None]
    for half in (1, 0):
        if half == 0:
            arrived(2)
        strided(0, 2 * half)
        strided(0, 2 * half + 1)
        halves[half] = dot(w1m[...], s[0, :, 256 * half : 256 * half + 256])
    pre = both[0:64] + jnp.concatenate(halves, axis=1)
    recv(S_B1, b1r, down, jnp.logical_not(first))
    pre = pre + jnp.where(first, 0.0, b1r[...])
    sl = jnp.where(pre > 0, 1.0, LEAK)
    group = act.at[rows(x * 64, 64), 128:640]
    group[...] = (pre * sl).astype(BF16)
    for k in range(3):
        send(S_ACT + k, group, group, xdev[k])
    slope[...] = sl

    recv(S_AGZ, azr, zdev)
    grad = az32[pl.ds(mine, 32)] + azr[...].astype(F32)
    pg2[0:32] = (grad * slope[pl.ds(mine, 32)]).astype(BF16)
    send(S_PG, pg2.at[0:32], pg2.at[32:64], down, jnp.logical_not(first))
    rfg[:, 1152:2304] = dot_t(pg2[0:32], s[0])
    rfg[:, 3456:3584] = jnp.zeros((32, 128), F32)
    recv(S_PG, pg2.at[32:64], up, jnp.logical_not(last))
    both = dot_t(pg2[...], s[1])
    rfg[:, 2304:3456] = both[0:32]
    rfg[:, 0:1152] = both[32:64]

    for k in range(32):
        low = rfg[:, 54 * k : 54 * k + 64]
        high = rfg[:, 54 * (k + 32) : 54 * (k + 32) + 64]
        tf[k % 2, (k % 8) // 2, k // 8] = jnp.concatenate([low, high], axis=1).astype(BF16)
    send(S_KF, tf.at[1 - core], cf, kdev)

    for k in range(3):
        recv(S_ACT + k, act.at[rows(lax.rem(x + 3 - k, NX) * 64, 64), 128:640], xdev[2 - k])
    recv(S_KF, cf, kdev)
    uf[...] = (tf[core].astype(F32) + cf[...].astype(F32)).astype(BF16)
    for k in range(3):
        send(S_YF + k, uf.at[lax.rem(y + k + 1, NY)], yf.at[k], ydev[k])
    for j in range(4):
        for kh in range(3):
            tile = shifted(act, j, kh)
            for kw in range(3):
                row = 256 * (3 * kh + kw)
                x9[row : row + 256, 128 * j : 128 * j + 128] = tile[:, 128 * kw : 128 * kw + 128]
    grads = dot_t(c3[:, 128:640], x9[...])
    rsg[0:32, 0:2304] = grads[0:32]
    rsg[0:32, 2304:3456] = grads[32:64, 0:1152]
    rsg[32:64, 0:1152] = grads[32:64, 1152:2304]
    rsg[32:64, 1152:3456] = grads[64:96]
    rsg[:, 3456:3584] = jnp.zeros((64, 128), F32)
    for k in range(32):
        piece = rsg[:, 108 * k : 108 * k + 128].astype(BF16)
        ts[k % 2, (k % 8) // 2, k // 8] = piece[0:32]
        ts[k % 2, (k % 8) // 2, k // 8 + 4] = piece[32:64]
    send(S_KS, ts.at[1 - core], cs, kdev)

    total = uf[y].astype(F32)
    for k in range(3):
        recv(S_YF + k, yf.at[k], ydev[2 - k])
        total = total + yf[k].astype(F32)
    vf[...] = total.astype(BF16)
    for k in range(7):
        send(S_ZF + k, vf.at[lax.rem(zl + k + 1, 4)], zf.at[k], zldev[k])

    recv(S_KS, cs, kdev)
    us[...] = (ts[core].astype(F32) + cs[...].astype(F32)).astype(BF16)
    for k in range(3):
        send(S_YS + k, us.at[lax.rem(y + k + 1, NY)], yg.at[k], ydev[k])

    out = dot(w2s[...], x9[...])
    ys[0:32] = out[0:32].astype(BF16)
    ys[32:64] = out[64:96].astype(BF16)
    send(S_Y, ys.at[0:32], yr.at[0], up, jnp.logical_not(last))
    send(S_Y + 1, ys.at[32:64], yr.at[1], down, jnp.logical_not(first))

    total = us[y].astype(F32)
    for k in range(3):
        recv(S_YS + k, yg.at[k], ydev[2 - k])
        total = total + yg[k].astype(F32)
    vs[...] = total.astype(BF16)
    for k in range(7):
        send(S_ZS + k, vs.at[lax.rem(zl + k + 1, NZ)], zs.at[k], zldev[k])

    recv(S_Y, yr.at[0], down, jnp.logical_not(first))
    recv(S_Y + 1, yr.at[1], up, jnp.logical_not(last))
    before = jnp.where(first, 0.0, yr[0].astype(F32))
    after = jnp.where(last, 0.0, yr[1].astype(F32))
    so[...] = (out[32:64] + before + after).astype(BF16)

    total = vf[lax.rem(zl, 4)].astype(F32)
    for k in range(7):
        recv(S_ZF + k, zf.at[k], zldev[6 - k])
        total = total + zf[k].astype(F32)
    fgo[...] = jnp.where(zl < 4, total[:, 0:54], total[:, 64:118])
    total = vs[zl].astype(F32)
    for k in range(7):
        recv(S_ZS + k, zs.at[k], zldev[6 - k])
        total = total + zs[k].astype(F32)
    sgo[...] = total[:, 0:108]

    for copy, cond in pending:
        if cond is None:
            copy.wait_send()
        else:
            pl.when(cond)(copy.wait_send)


def shards(sample, first_weight, second_weight, cotangent):
    vmem = pl.BlockSpec(memory_space=pltpu.VMEM)
    hbm = pl.BlockSpec(memory_space=pltpu.HBM)
    b16 = [
        (16, 2, 16, 128), (32, 3456), (32, 6912), (32, 1, 8, 64), (32, 16, 128), (32, 512), (33, 128, 128),
        (2, 1152, 512), (96, 768), (864, 512), (864, 256),
    ]
    scratch = [pltpu.VMEM(shape, BF16) for shape in b16]
    scratch += [pltpu.VMEM((256, 512), F32)]
    scratch += [pltpu.VMEM((256, 512), BF16), pltpu.VMEM((3, 64, 512), BF16), pltpu.VMEM((64, 512), F32)]
    scratch += [pltpu.VMEM((64, 512), BF16), pltpu.VMEM((32, 512), BF16)]
    scratch += [pltpu.VMEM((4, 2, 7, 16, 128), BF16)] * 2
    scratch += [pltpu.VMEM((128, 1152), BF16), pltpu.VMEM((64, 1152), BF16)]
    scratch += [pltpu.VMEM((64, 512), F32)] * 3
    scratch += [pltpu.VMEM(shape, BF16) for shape in ((256, 768), (64, 512), (2304, 512), (96, 2304), (64, 512), (2, 32, 512))]
    scratch += [pltpu.VMEM((64, 3584), F32), pltpu.VMEM((32, 3584), F32)]
    for n in (4, 8):
        shapes = ((2, 4, n), (4, n), (4, n), (3, n), (n,), (7,))
        scratch += [pltpu.VMEM(shape + (32, 128), BF16) for shape in shapes]
    scratch += [pltpu.SemaphoreType.DMA((N_SEM,))] * 2 + [pltpu.SemaphoreType.DMA((4,))]
    so, fgo, sgo = pl.pallas_call(
        kernel,
        out_shape=(
            jax.ShapeDtypeStruct((32, 512), BF16),
            jax.ShapeDtypeStruct((32, 54), F32),
            jax.ShapeDtypeStruct((32, 108), F32),
        ),
        in_specs=[hbm] * 4,
        out_specs=(vmem, vmem, vmem),
        scratch_shapes=scratch,
        compiler_params=pltpu.CompilerParams(collective_id=0, has_side_effects=True, vmem_limit_bytes=VMEM_BYTES),
        name="slab_pair",
    )(sample, first_weight, second_weight, cotangent)
    return so.reshape(32, 1, 8, 64), fgo, sgo


def solution(mesh):
    return jax.shard_map(
        shards,
        mesh=mesh,
        in_specs=(
            P("chan", "depth", None, None),
            P("chan", None),
            P("chan", None),
            P("chan", "depth", None, None),
        ),
        out_specs=(P("chan", "depth", None, None), P("chan", "depth"), P("chan", "depth")),
        check_vma=False,
    )
```

```python
import jax
import jax.numpy as jnp
from jax import lax
from jax.experimental import pallas as pl
from jax.experimental.pallas import tpu as pltpu
from jax.sharding import PartitionSpec as P

LEAK = 0.3
F32 = jnp.float32
BF16 = jnp.bfloat16
MESH = pl.DeviceIdType.MESH

NZ, NY, NK, NX = 8, 4, 2, 4
DEPTH = NZ * NY * NK

S_Z = 0
S_OX = 3
S_FX = 9
S_ACT = 18
S_COT = 21
S_AGX = 23
S_AGZ = 26
S_B1 = 27
S_PG = 28
S_Y = 29
S_KF = 31
S_KS = 32
S_YF = 33
S_YS = 36
S_ZF = 39
S_ZS = 46
S_WZ = 53
S_WY = 54
S_WK = 57
N_SEM = 58

VMEM_BYTES = 64 * 1024 * 1024 - 16 * 1024

CHUNKS = ((16, 32), (7, 16), (0, 7))


def dot(a, b):
    return lax.dot_general(a, b, (((1,), (0,)), ((), ())), preferred_element_type=F32)


def dot_t(a, b):
    return lax.dot_general(a, b, (((1,), (1,)), ((), ())), preferred_element_type=F32)


def shift_matrix(rows, base):
    r = lax.broadcasted_iota(jnp.int32, (rows, 384), 0)
    c = lax.broadcasted_iota(jnp.int32, (rows, 384), 1)
    kw = c >> 7
    m = c & 127
    w = (m & 63) + kw - 1
    hit = (r == m + base + kw - 1) & (w >= 0) & (w < 64)
    return jnp.where(hit, 1.0, 0.0).astype(BF16)


def stride_matrix():
    r = lax.broadcasted_iota(jnp.int32, (256, 384), 0)
    c = lax.broadcasted_iota(jnp.int32, (256, 384), 1)
    kw = c >> 7
    i = (c >> 6) & 1
    w = 2 * (c & 63) + kw - 1
    hit = (r == i * 128 + w) & (w >= 0)
    return jnp.where(hit, 1.0, 0.0).astype(BF16)


def swap_matrix(rows, fast):
    slow = rows // fast
    bits = slow.bit_length() - 1
    r = lax.broadcasted_iota(jnp.int32, (rows, rows), 0)
    k = lax.broadcasted_iota(jnp.int32, (rows, rows), 1)
    hit = ((k >> bits) == (r & (fast - 1))) & ((k & (slow - 1)) == (r >> (fast.bit_length() - 1)))
    return jnp.where(hit, 1.0, 0.0).astype(BF16)


def kernel(
    samp_hbm, w1_hbm, w2_hbm, cot_hbm,
    so, fgo, sgo,
    sraw, w1, w2, craw, own, cot, g, s, c3, ci, wv, ag32, agb, agr, az32, azb, azr, wo, wp, w1p, w1m, b1s, b1r,
    slope, act, pg2, x9, w2s, ys, yr, rsg, rfg, tf, cf, uf, yf, vf, zf, ts, cs, us, yg, vs, zs,
    send_sems, recv_sems, load_sems,
):
    d = lax.axis_index("depth")
    c = lax.axis_index("chan")
    core = lax.rem(d, 2)
    y = lax.rem(d // 2, NY)
    zl = d // (2 * NY)
    x = c // 2
    zh = lax.rem(c, 2)
    first = d == 0
    last = d == DEPTH - 1

    def chan_at(dx, flip=False):
        return lax.rem(x + dx + NX, NX) * 2 + (1 - zh if flip else zh)

    xdev = [(d, chan_at(k)) for k in (1, 2, 3)]
    zdev = (d, chan_at(0, True))
    kdev = (d + 1 - 2 * core, c)
    ydev = [(zl * 8 + lax.rem(y + k, NY) * 2 + core, c) for k in (1, 2, 3)]
    zldev = [(lax.rem(zl + k, NZ) * 8 + y * 2 + core, c) for k in range(1, 8)]
    up = (lax.rem(d + 1, DEPTH), c)
    down = (lax.rem(d + DEPTH - 1, DEPTH), c)

    barrier = pltpu.get_barrier_semaphore()
    partners = [zdev] + zldev + xdev + ydev + [kdev, up, down]
    for dev in partners:
        pl.semaphore_signal(barrier, inc=1, device_id=dev, device_id_type=MESH)
    loads = [
        pltpu.make_async_copy(src, dst, load_sems.at[i])
        for i, (src, dst) in enumerate(((samp_hbm, sraw), (cot_hbm, craw), (w1_hbm, w1), (w2_hbm, w2)))
    ]
    for load in loads:
        load.start()

    pending = []

    def desc(k, src, dst, dev):
        return pltpu.make_async_remote_copy(
            src_ref=src, dst_ref=dst, send_sem=send_sems.at[k], recv_sem=recv_sems.at[k], device_id=dev, device_id_type=MESH
        )

    def send(k, src, dst, dev, cond=None):
        copy = desc(k, src, dst, dev)
        if cond is None:
            copy.start()
        else:
            pl.when(cond)(copy.start)
        pending.append((copy, cond))

    def recv(k, dst, dev, cond=None):
        copy = desc(k, dst, dst, dev)
        if cond is None:
            copy.wait_recv()
        else:
            pl.when(cond)(copy.wait_recv)

    def rows(start, size):
        return pl.ds(pl.multiple_of(start, size), size)

    def sample_block(r, lines):
        return g.at[lines[0] : lines[1], rows(r * 16, 16), :]

    loads[0].wait()
    swap = swap_matrix(256, 16)
    for plane in range(2):
        lines = dot(swap, sraw[:, plane].reshape(256, 128))
        own[16 * plane : 16 * plane + 16] = lines.astype(BF16).reshape(16, 16, 128)
    loads[1].wait()
    lines = dot(swap_matrix(256, 32), craw[:, 0].astype(F32).reshape(256, 64).astype(BF16))
    for j in range(4):
        pair = jnp.concatenate([lines[64 * j : 64 * j + 32], lines[64 * j + 32 : 64 * j + 64]], axis=1)
        cot[:, 128 * j : 128 * j + 128] = pair.astype(BF16)
    loads[2].wait()
    wo[3, 1] = jnp.zeros((7, 16, 128), BF16)
    for k in range(54):
        at = 16 * (k % 2)
        wo[k // 14, k // 7 % 2, k % 7] = w1[at : at + 16, 128 * (k // 2) : 128 * (k // 2) + 128]
    pl.semaphore_wait(barrier, len(partners))

    send(S_WZ, wo.at[y, core], wp.at[y, core], zdev)
    over = [desc(S_Z + i, own.at[a:b], sample_block(c, (a, b)), zdev) for i, (a, b) in enumerate(CHUNKS)]
    over[0].start()
    send(S_COT, cot, c3.at[64:96, 128:640], up, jnp.logical_not(last))
    send(S_COT + 1, cot, c3.at[0:32, 128:640], down, jnp.logical_not(first))
    for i, lines in enumerate(((16, 32), (0, 16))):
        for k in range(3):
            send(S_OX + 3 * i + k, own.at[lines[0] : lines[1]], sample_block(c, lines), xdev[k])

    c3[:, 0:128] = jnp.zeros((96, 128), BF16)
    c3[:, 640:768] = jnp.zeros((96, 128), BF16)
    act[:, 0:128] = jnp.zeros((256, 128), BF16)
    act[:, 640:768] = jnp.zeros((256, 128), BF16)
    g[32] = jnp.zeros((128, 128), BF16)

    @pl.when(first)
    def _():
        c3[64:96, 128:640] = jnp.zeros((32, 512), BF16)

    @pl.when(last)
    def _():
        c3[0:32, 128:640] = jnp.zeros((32, 512), BF16)
        pg2[32:64] = jnp.zeros((32, 512), BF16)

    c3[32:64, 128:640] = cot[...]
    g[0:32, rows(c * 16, 16), :] = own[...]
    loads[3].wait()
    for k in range(27):
        wv[32 * k : 32 * k + 32] = w2[:, 256 * k : 256 * k + 256]
    for k in range(3):
        w2s[32 * k : 32 * k + 32] = w2[:, 2304 * k : 2304 * k + 2304]
    mine = pl.multiple_of(zh * 32, 32)
    theirs = pl.multiple_of((1 - zh) * 32, 32)
    w1p[pl.ds(mine, 32)] = w1[:, 2304:3456]
    w1p[pl.ds(mine + 64, 32)] = w1[:, 0:1152]
    w1m[pl.ds(mine, 32)] = w1[:, 1152:2304]
    sh_two = shift_matrix(256, 64)
    sh_one = shift_matrix(128, 0)
    recv(S_COT, c3.at[64:96, 128:640], down, jnp.logical_not(first))
    recv(S_COT + 1, c3.at[0:32, 128:640], up, jnp.logical_not(last))

    def shifted(ref, j, kh):
        if kh == 1:
            return dot(ref[:, 128 * (j + 1) : 128 * (j + 2)], sh_one).astype(BF16)
        at = 128 * j if kh == 0 else 128 * (j + 1)
        return dot(ref[:, at : at + 256], sh_two).astype(BF16)

    for j in range(4):
        for kh in range(3):
            tile = shifted(c3, j, kh)
            for kw in range(3):
                for kd in range(3):
                    tap = 9 * kd + 3 * (2 - kh) + 2 - kw
                    ci[32 * tap : 32 * tap + 32, 128 * j : 128 * j + 128] = tile[32 * kd : 32 * kd + 32, 128 * kw : 128 * kw + 128]
    part = lax.dot_general(wv[...], ci[...], (((0,), (0,)), ((), ())), preferred_element_type=F32)
    ag32[...] = part
    agb[...] = part.astype(BF16)
    for k in range(3):
        send(S_AGX + k, agb.at[rows(lax.rem(x + k + 1, NX) * 64, 64)], agr.at[k], xdev[k])

    over[0].wait_send()
    over[1].start()
    recv(S_WZ, wp.at[y, core], zdev)
    for k in range(3):
        send(S_WY + k, wp.at[y, core], wp.at[y, core], ydev[k])

    over[1].wait_send()
    over[2].start()
    total = ag32[rows(x * 64, 64)]
    for k in range(3):
        recv(S_AGX + k, agr.at[k], xdev[2 - k])
        total = total + agr[k].astype(F32)
    az32[...] = total
    azb[...] = total.astype(BF16)
    over[2].wait_send()
    send(S_AGZ, azb.at[pl.ds(theirs, 32)], azr, zdev)

    def across(i):
        block = sample_block(chan_at(0, True), CHUNKS[i])
        recv(S_Z + i, block, zdev)
        for k in range(3):
            send(S_FX + 3 * i + k, block, block, xdev[k])

    def arrived(i):
        for k in range(3):
            recv(S_FX + 3 * i + k, sample_block(chan_at(3 - k, True), CHUNKS[i]), xdev[2 - k])

    across(0)
    for k in range(3):
        recv(S_WY + k, wp.at[lax.rem(y + 3 - k, NY), core], ydev[2 - k])
    send(S_WK, wp.at[:, core], wp.at[:, core], kdev)
    across(1)
    for i, lines in enumerate(((16, 32), (0, 16))):
        for k in range(3):
            recv(S_OX + 3 * i + k, sample_block(chan_at(3 - k), lines), xdev[2 - k])
    stride = stride_matrix()

    def strided(plane, j):
        for kh in range(3):
            at = 4 * j + kh - 1
            low = g[16 * plane + at] if at >= 0 else g[32]
            tile = dot(jnp.concatenate([low, g[16 * plane + at + 2]], axis=1), stride).astype(BF16)
            for kw in range(3):
                row = 128 * (3 * kh + kw)
                s[plane, row : row + 128, 128 * j : 128 * j + 128] = tile[:, 128 * kw : 128 * kw + 128]

    arrived(0)
    for j in range(4):
        strided(1, j)
    recv(S_WK, wp.at[:, 1 - core], kdev)
    for k in range(54):
        tile = wp[k // 14, k // 7 % 2, k % 7]
        at = 128 * (k // 2 % 9)
        row = theirs + 16 * (k % 2)
        if k // 18 == 1:
            w1m[pl.ds(row, 16), at : at + 128] = tile
        else:
            w1p[pl.ds(row + (64 if k < 18 else 0), 16), at : at + 128] = tile
    both = dot(w1p[...], s[1])
    b1s[...] = both[64:128]
    send(S_B1, b1s, b1r, up, jnp.logical_not(last))
    across(2)
    arrived(1)
    halves = [None, None]
    for half in (1, 0):
        if half == 0:
            arrived(2)
        strided(0, 2 * half)
        strided(0, 2 * half + 1)
        halves[half] = dot(w1m[...], s[0, :, 256 * half : 256 * half + 256])
    pre = both[0:64] + jnp.concatenate(halves, axis=1)
    recv(S_B1, b1r, down, jnp.logical_not(first))
    pre = pre + jnp.where(first, 0.0, b1r[...])
    sl = jnp.where(pre > 0, 1.0, LEAK)
    group = act.at[rows(x * 64, 64), 128:640]
    group[...] = (pre * sl).astype(BF16)
    for k in (1, 0, 2):
        send(S_ACT + k, group, group, xdev[k])
    slope[...] = sl

    recv(S_AGZ, azr, zdev)
    grad = az32[pl.ds(mine, 32)] + azr[...].astype(F32)
    pg2[0:32] = (grad * slope[pl.ds(mine, 32)]).astype(BF16)
    send(S_PG, pg2.at[0:32], pg2.at[32:64], down, jnp.logical_not(first))
    rfg[:, 1152:2304] = dot_t(pg2[0:32], s[0])
    rfg[:, 3456:3584] = jnp.zeros((32, 128), F32)
    recv(S_PG, pg2.at[32:64], up, jnp.logical_not(last))
    both = dot_t(pg2[...], s[1])
    rfg[:, 2304:3456] = both[0:32]
    rfg[:, 0:1152] = both[32:64]

    for k in range(32):
        low = rfg[:, 54 * k : 54 * k + 64]
        high = rfg[:, 54 * (k + 32) : 54 * (k + 32) + 64]
        tf[k % 2, (k % 8) // 2, k // 8] = jnp.concatenate([low, high], axis=1).astype(BF16)
    send(S_KF, tf.at[1 - core], cf, kdev)

    for k in range(3):
        recv(S_ACT + k, act.at[rows(lax.rem(x + 3 - k, NX) * 64, 64), 128:640], xdev[2 - k])
    recv(S_KF, cf, kdev)
    uf[...] = (tf[core].astype(F32) + cf[...].astype(F32)).astype(BF16)
    for k in range(3):
        send(S_YF + k, uf.at[lax.rem(y + k + 1, NY)], yf.at[k], ydev[k])
    for j in range(4):
        for kh in range(3):
            tile = shifted(act, j, kh)
            for kw in range(3):
                row = 256 * (3 * kh + kw)
                x9[row : row + 256, 128 * j : 128 * j + 128] = tile[:, 128 * kw : 128 * kw + 128]
    grads = dot_t(c3[:, 128:640], x9[...])
    rsg[0:32, 0:2304] = grads[0:32]
    rsg[0:32, 2304:3456] = grads[32:64, 0:1152]
    rsg[32:64, 0:1152] = grads[32:64, 1152:2304]
    rsg[32:64, 1152:3456] = grads[64:96]
    rsg[:, 3456:3584] = jnp.zeros((64, 128), F32)
    for k in range(32):
        piece = rsg[:, 108 * k : 108 * k + 128].astype(BF16)
        ts[k % 2, (k % 8) // 2, k // 8] = piece[0:32]
        ts[k % 2, (k % 8) // 2, k // 8 + 4] = piece[32:64]
    send(S_KS, ts.at[1 - core], cs, kdev)

    recv(S_KS, cs, kdev)
    us[...] = (ts[core].astype(F32) + cs[...].astype(F32)).astype(BF16)
    for k in (1, 0, 2):
        send(S_YS + k, us.at[lax.rem(y + k + 1, NY)], yg.at[k], ydev[k])

    out = dot(w2s[...], x9[...])
    ys[0:32] = out[0:32].astype(BF16)
    ys[32:64] = out[64:96].astype(BF16)

    total = uf[y].astype(F32)
    for k in range(3):
        recv(S_YF + k, yf.at[k], ydev[2 - k])
        total = total + yf[k].astype(F32)
    vf[...] = total.astype(BF16)
    for k in range(7):
        send(S_ZF + k, vf.at[lax.rem(zl + k + 1, 4)], zf.at[k], zldev[k])

    total = us[y].astype(F32)
    for k in range(3):
        recv(S_YS + k, yg.at[k], ydev[2 - k])
        total = total + yg[k].astype(F32)
    vs[...] = total.astype(BF16)
    for k in range(7):
        send(S_ZS + k, vs.at[lax.rem(zl + k + 1, NZ)], zs.at[k], zldev[k])

    send(S_Y, ys.at[0:32], yr.at[0], up, jnp.logical_not(last))
    send(S_Y + 1, ys.at[32:64], yr.at[1], down, jnp.logical_not(first))
    recv(S_Y, yr.at[0], down, jnp.logical_not(first))
    recv(S_Y + 1, yr.at[1], up, jnp.logical_not(last))
    before = jnp.where(first, 0.0, yr[0].astype(F32))
    after = jnp.where(last, 0.0, yr[1].astype(F32))
    so[...] = (out[32:64] + before + after).astype(BF16)

    total = vf[lax.rem(zl, 4)].astype(F32)
    for k in range(7):
        recv(S_ZF + k, zf.at[k], zldev[6 - k])
        total = total + zf[k].astype(F32)
    fgo[...] = jnp.where(zl < 4, total[:, 0:54], total[:, 64:118])
    total = vs[zl].astype(F32)
    for k in range(7):
        recv(S_ZS + k, zs.at[k], zldev[6 - k])
        total = total + zs[k].astype(F32)
    sgo[...] = total[:, 0:108]

    for copy, cond in pending:
        if cond is None:
            copy.wait_send()
        else:
            pl.when(cond)(copy.wait_send)


def shards(sample, first_weight, second_weight, cotangent):
    vmem = pl.BlockSpec(memory_space=pltpu.VMEM)
    hbm = pl.BlockSpec(memory_space=pltpu.HBM)
    b16 = [
        (16, 2, 16, 128), (32, 3456), (32, 6912), (32, 1, 8, 64), (32, 16, 128), (32, 512), (33, 128, 128),
        (2, 1152, 512), (96, 768), (864, 512), (864, 256),
    ]
    scratch = [pltpu.VMEM(shape, BF16) for shape in b16]
    scratch += [pltpu.VMEM((256, 512), F32)]
    scratch += [pltpu.VMEM((256, 512), BF16), pltpu.VMEM((3, 64, 512), BF16), pltpu.VMEM((64, 512), F32)]
    scratch += [pltpu.VMEM((64, 512), BF16), pltpu.VMEM((32, 512), BF16)]
    scratch += [pltpu.VMEM((4, 2, 7, 16, 128), BF16)] * 2
    scratch += [pltpu.VMEM((128, 1152), BF16), pltpu.VMEM((64, 1152), BF16)]
    scratch += [pltpu.VMEM((64, 512), F32)] * 3
    scratch += [pltpu.VMEM(shape, BF16) for shape in ((256, 768), (64, 512), (2304, 512), (96, 2304), (64, 512), (2, 32, 512))]
    scratch += [pltpu.VMEM((64, 3584), F32), pltpu.VMEM((32, 3584), F32)]
    for n in (4, 8):
        shapes = ((2, 4, n), (4, n), (4, n), (3, n), (n,), (7,))
        scratch += [pltpu.VMEM(shape + (32, 128), BF16) for shape in shapes]
    scratch += [pltpu.SemaphoreType.DMA((N_SEM,))] * 2 + [pltpu.SemaphoreType.DMA((4,))]
    so, fgo, sgo = pl.pallas_call(
        kernel,
        out_shape=(
            jax.ShapeDtypeStruct((32, 512), BF16),
            jax.ShapeDtypeStruct((32, 54), F32),
            jax.ShapeDtypeStruct((32, 108), F32),
        ),
        in_specs=[hbm] * 4,
        out_specs=(vmem, vmem, vmem),
        scratch_shapes=scratch,
        compiler_params=pltpu.CompilerParams(collective_id=0, has_side_effects=True, vmem_limit_bytes=VMEM_BYTES),
        name="slab_pair",
    )(sample, first_weight, second_weight, cotangent)
    return so.reshape(32, 1, 8, 64), fgo, sgo


def solution(mesh):
    return jax.shard_map(
        shards,
        mesh=mesh,
        in_specs=(
            P("chan", "depth", None, None),
            P("chan", None),
            P("chan", None),
            P("chan", "depth", None, None),
        ),
        out_specs=(P("chan", "depth", None, None), P("chan", "depth"), P("chan", "depth")),
        check_vma=False,
    )
```

```python
import jax
import jax.numpy as jnp
from jax import lax
from jax.experimental import pallas as pl
from jax.experimental.pallas import tpu as pltpu
from jax.sharding import PartitionSpec as P

LEAK = 0.3
F32 = jnp.float32
BF16 = jnp.bfloat16
MESH = pl.DeviceIdType.MESH

NZ, NY, NK, NX = 8, 4, 2, 4
DEPTH = NZ * NY * NK

S_Z = 0
S_OX = 3
S_FX = 9
S_ACT = 18
S_COT = 21
S_AGX = 23
S_AGZ = 26
S_B1 = 27
S_PG = 28
S_Y = 29
S_KF = 31
S_KS = 32
S_YF = 33
S_YS = 36
S_ZF = 39
S_ZS = 46
S_WZ = 53
S_WY = 54
S_WK = 57
N_SEM = 58

VMEM_BYTES = 64 * 1024 * 1024 - 16 * 1024

CHUNKS = ((16, 32), (7, 16), (0, 7))


def dot(a, b):
    return lax.dot_general(a, b, (((1,), (0,)), ((), ())), preferred_element_type=F32)


def dot_t(a, b):
    return lax.dot_general(a, b, (((1,), (1,)), ((), ())), preferred_element_type=F32)


def shift_matrix(rows, base):
    r = lax.broadcasted_iota(jnp.int32, (rows, 384), 0)
    c = lax.broadcasted_iota(jnp.int32, (rows, 384), 1)
    kw = c >> 7
    m = c & 127
    w = (m & 63) + kw - 1
    hit = (r == m + base + kw - 1) & (w >= 0) & (w < 64)
    return jnp.where(hit, 1.0, 0.0).astype(BF16)


def stride_matrix():
    r = lax.broadcasted_iota(jnp.int32, (256, 384), 0)
    c = lax.broadcasted_iota(jnp.int32, (256, 384), 1)
    kw = c >> 7
    i = (c >> 6) & 1
    w = 2 * (c & 63) + kw - 1
    hit = (r == i * 128 + w) & (w >= 0)
    return jnp.where(hit, 1.0, 0.0).astype(BF16)


def swap_matrix(rows, fast):
    slow = rows // fast
    bits = slow.bit_length() - 1
    r = lax.broadcasted_iota(jnp.int32, (rows, rows), 0)
    k = lax.broadcasted_iota(jnp.int32, (rows, rows), 1)
    hit = ((k >> bits) == (r & (fast - 1))) & ((k & (slow - 1)) == (r >> (fast.bit_length() - 1)))
    return jnp.where(hit, 1.0, 0.0).astype(BF16)


def kernel(
    samp_hbm, w1_hbm, w2_hbm, cot_hbm,
    so, fgo, sgo,
    sraw, w1, w2, craw, own, cot, g, s, c3, ci, wv, ag32, agb, agr, az32, azb, azr, wo, wp, w1p, w1m, b1s, b1r,
    slope, act, pg2, x9, w2s, ys, yr, rsg, rfg, tf, cf, uf, yf, vf, zf, ts, cs, us, yg, vs, zs,
    send_sems, recv_sems, load_sems,
):
    d = lax.axis_index("depth")
    c = lax.axis_index("chan")
    core = lax.rem(d, 2)
    y = lax.rem(d // 2, NY)
    zl = d // (2 * NY)
    x = c // 2
    zh = lax.rem(c, 2)
    first = d == 0
    last = d == DEPTH - 1

    def chan_at(dx, flip=False):
        return lax.rem(x + dx + NX, NX) * 2 + (1 - zh if flip else zh)

    xdev = [(d, chan_at(k)) for k in (1, 2, 3)]
    zdev = (d, chan_at(0, True))
    kdev = (d + 1 - 2 * core, c)
    ydev = [(zl * 8 + lax.rem(y + k, NY) * 2 + core, c) for k in (1, 2, 3)]
    zldev = [(lax.rem(zl + k, NZ) * 8 + y * 2 + core, c) for k in range(1, 8)]
    up = (lax.rem(d + 1, DEPTH), c)
    down = (lax.rem(d + DEPTH - 1, DEPTH), c)

    barrier = pltpu.get_barrier_semaphore()
    partners = [zdev] + zldev + xdev + ydev + [kdev, up, down]
    for dev in partners:
        pl.semaphore_signal(barrier, inc=1, device_id=dev, device_id_type=MESH)
    loads = [
        pltpu.make_async_copy(src, dst, load_sems.at[i])
        for i, (src, dst) in enumerate(((samp_hbm, sraw), (cot_hbm, craw), (w1_hbm, w1), (w2_hbm, w2)))
    ]
    for load in loads:
        load.start()

    pending = []

    def desc(k, src, dst, dev):
        return pltpu.make_async_remote_copy(
            src_ref=src, dst_ref=dst, send_sem=send_sems.at[k], recv_sem=recv_sems.at[k], device_id=dev, device_id_type=MESH
        )

    def send(k, src, dst, dev, cond=None):
        copy = desc(k, src, dst, dev)
        if cond is None:
            copy.start()
        else:
            pl.when(cond)(copy.start)
        pending.append((copy, cond))

    def recv(k, dst, dev, cond=None):
        copy = desc(k, dst, dst, dev)
        if cond is None:
            copy.wait_recv()
        else:
            pl.when(cond)(copy.wait_recv)

    def rows(start, size):
        return pl.ds(pl.multiple_of(start, size), size)

    def sample_block(r, lines):
        return g.at[lines[0] : lines[1], rows(r * 16, 16), :]

    loads[0].wait()
    swap = swap_matrix(256, 16)
    for plane in range(2):
        lines = dot(swap, sraw[:, plane].reshape(256, 128))
        own[16 * plane : 16 * plane + 16] = lines.astype(BF16).reshape(16, 16, 128)
    loads[1].wait()
    lines = dot(swap_matrix(256, 32), craw[:, 0].astype(F32).reshape(256, 64).astype(BF16))
    for j in range(4):
        pair = jnp.concatenate([lines[64 * j : 64 * j + 32], lines[64 * j + 32 : 64 * j + 64]], axis=1)
        cot[:, 128 * j : 128 * j + 128] = pair.astype(BF16)
    loads[2].wait()
    wo[3, 1] = jnp.zeros((7, 16, 128), BF16)
    for k in range(54):
        at = 16 * (k % 2)
        wo[k // 14, k // 7 % 2, k % 7] = w1[at : at + 16, 128 * (k // 2) : 128 * (k // 2) + 128]
    pl.semaphore_wait(barrier, len(partners))

    send(S_WZ, wo.at[y, core], wp.at[y, core], zdev)
    over = [desc(S_Z + i, own.at[a:b], sample_block(c, (a, b)), zdev) for i, (a, b) in enumerate(CHUNKS)]
    over[0].start()
    send(S_COT, cot, c3.at[64:96, 128:640], up, jnp.logical_not(last))
    send(S_COT + 1, cot, c3.at[0:32, 128:640], down, jnp.logical_not(first))
    for i, lines in enumerate(((16, 32), (0, 16))):
        for k in (1, 0, 2):
            send(S_OX + 3 * i + k, own.at[lines[0] : lines[1]], sample_block(c, lines), xdev[k])

    c3[:, 0:128] = jnp.zeros((96, 128), BF16)
    c3[:, 640:768] = jnp.zeros((96, 128), BF16)
    act[:, 0:128] = jnp.zeros((256, 128), BF16)
    act[:, 640:768] = jnp.zeros((256, 128), BF16)
    g[32] = jnp.zeros((128, 128), BF16)

    @pl.when(first)
    def _():
        c3[64:96, 128:640] = jnp.zeros((32, 512), BF16)

    @pl.when(last)
    def _():
        c3[0:32, 128:640] = jnp.zeros((32, 512), BF16)
        pg2[32:64] = jnp.zeros((32, 512), BF16)

    c3[32:64, 128:640] = cot[...]
    g[0:32, rows(c * 16, 16), :] = own[...]
    loads[3].wait()
    for k in range(27):
        wv[32 * k : 32 * k + 32] = w2[:, 256 * k : 256 * k + 256]
    for k in range(3):
        w2s[32 * k : 32 * k + 32] = w2[:, 2304 * k : 2304 * k + 2304]
    mine = pl.multiple_of(zh * 32, 32)
    theirs = pl.multiple_of((1 - zh) * 32, 32)
    w1p[pl.ds(mine, 32)] = w1[:, 2304:3456]
    w1p[pl.ds(mine + 64, 32)] = w1[:, 0:1152]
    w1m[pl.ds(mine, 32)] = w1[:, 1152:2304]
    sh_two = shift_matrix(256, 64)
    sh_one = shift_matrix(128, 0)
    recv(S_COT, c3.at[64:96, 128:640], down, jnp.logical_not(first))
    recv(S_COT + 1, c3.at[0:32, 128:640], up, jnp.logical_not(last))

    def shifted(ref, j, kh):
        if kh == 1:
            return dot(ref[:, 128 * (j + 1) : 128 * (j + 2)], sh_one).astype(BF16)
        at = 128 * j if kh == 0 else 128 * (j + 1)
        return dot(ref[:, at : at + 256], sh_two).astype(BF16)

    for j in range(4):
        for kh in range(3):
            tile = shifted(c3, j, kh)
            for kw in range(3):
                for kd in range(3):
                    tap = 9 * kd + 3 * (2 - kh) + 2 - kw
                    ci[32 * tap : 32 * tap + 32, 128 * j : 128 * j + 128] = tile[32 * kd : 32 * kd + 32, 128 * kw : 128 * kw + 128]
    part = lax.dot_general(wv[...], ci[...], (((0,), (0,)), ((), ())), preferred_element_type=F32)
    ag32[...] = part
    agb[...] = part.astype(BF16)
    for k in (1, 0, 2):
        send(S_AGX + k, agb.at[rows(lax.rem(x + k + 1, NX) * 64, 64)], agr.at[k], xdev[k])

    over[0].wait_send()
    over[1].start()
    recv(S_WZ, wp.at[y, core], zdev)
    for k in range(3):
        send(S_WY + k, wp.at[y, core], wp.at[y, core], ydev[k])

    over[1].wait_send()
    over[2].start()
    total = ag32[rows(x * 64, 64)]
    for k in range(3):
        recv(S_AGX + k, agr.at[k], xdev[2 - k])
        total = total + agr[k].astype(F32)
    az32[...] = total
    azb[...] = total.astype(BF16)
    over[2].wait_send()
    send(S_AGZ, azb.at[pl.ds(theirs, 32)], azr, zdev)

    def across(i):
        block = sample_block(chan_at(0, True), CHUNKS[i])
        recv(S_Z + i, block, zdev)
        for k in (1, 0, 2):
            send(S_FX + 3 * i + k, block, block, xdev[k])

    def arrived(i):
        for k in range(3):
            recv(S_FX + 3 * i + k, sample_block(chan_at(3 - k, True), CHUNKS[i]), xdev[2 - k])

    across(0)
    for k in range(3):
        recv(S_WY + k, wp.at[lax.rem(y + 3 - k, NY), core], ydev[2 - k])
    send(S_WK, wp.at[:, core], wp.at[:, core], kdev)
    across(1)
    for i, lines in enumerate(((16, 32), (0, 16))):
        for k in range(3):
            recv(S_OX + 3 * i + k, sample_block(chan_at(3 - k), lines), xdev[2 - k])
    stride = stride_matrix()

    def strided(plane, j):
        for kh in range(3):
            at = 4 * j + kh - 1
            low = g[16 * plane + at] if at >= 0 else g[32]
            tile = dot(jnp.concatenate([low, g[16 * plane + at + 2]], axis=1), stride).astype(BF16)
            for kw in range(3):
                row = 128 * (3 * kh + kw)
                s[plane, row : row + 128, 128 * j : 128 * j + 128] = tile[:, 128 * kw : 128 * kw + 128]

    arrived(0)
    for j in range(4):
        strided(1, j)
    recv(S_WK, wp.at[:, 1 - core], kdev)
    for k in range(54):
        tile = wp[k // 14, k // 7 % 2, k % 7]
        at = 128 * (k // 2 % 9)
        row = theirs + 16 * (k % 2)
        if k // 18 == 1:
            w1m[pl.ds(row, 16), at : at + 128] = tile
        else:
            w1p[pl.ds(row + (64 if k < 18 else 0), 16), at : at + 128] = tile
    both = dot(w1p[...], s[1])
    b1s[...] = both[64:128]
    send(S_B1, b1s, b1r, up, jnp.logical_not(last))
    across(2)
    arrived(1)
    halves = [None, None]
    for half in (1, 0):
        if half == 0:
            arrived(2)
        strided(0, 2 * half)
        strided(0, 2 * half + 1)
        halves[half] = dot(w1m[...], s[0, :, 256 * half : 256 * half + 256])
    pre = both[0:64] + jnp.concatenate(halves, axis=1)
    recv(S_B1, b1r, down, jnp.logical_not(first))
    pre = pre + jnp.where(first, 0.0, b1r[...])
    sl = jnp.where(pre > 0, 1.0, LEAK)
    group = act.at[rows(x * 64, 64), 128:640]
    group[...] = (pre * sl).astype(BF16)
    for k in (1, 0, 2):
        send(S_ACT + k, group, group, xdev[k])
    slope[...] = sl

    recv(S_AGZ, azr, zdev)
    grad = az32[pl.ds(mine, 32)] + azr[...].astype(F32)
    pg2[0:32] = (grad * slope[pl.ds(mine, 32)]).astype(BF16)
    send(S_PG, pg2.at[0:32], pg2.at[32:64], down, jnp.logical_not(first))
    rfg[:, 1152:2304] = dot_t(pg2[0:32], s[0])
    rfg[:, 3456:3584] = jnp.zeros((32, 128), F32)
    recv(S_PG, pg2.at[32:64], up, jnp.logical_not(last))
    both = dot_t(pg2[...], s[1])
    rfg[:, 2304:3456] = both[0:32]
    rfg[:, 0:1152] = both[32:64]

    for k in range(32):
        low = rfg[:, 54 * k : 54 * k + 64]
        high = rfg[:, 54 * (k + 32) : 54 * (k + 32) + 64]
        tf[k % 2, (k % 8) // 2, k // 8] = jnp.concatenate([low, high], axis=1).astype(BF16)
    send(S_KF, tf.at[1 - core], cf, kdev)

    for k in range(3):
        recv(S_ACT + k, act.at[rows(lax.rem(x + 3 - k, NX) * 64, 64), 128:640], xdev[2 - k])
    recv(S_KF, cf, kdev)
    uf[...] = (tf[core].astype(F32) + cf[...].astype(F32)).astype(BF16)
    for k in (1, 0, 2):
        send(S_YF + k, uf.at[lax.rem(y + k + 1, NY)], yf.at[k], ydev[k])
    for j in range(4):
        for kh in range(3):
            tile = shifted(act, j, kh)
            for kw in range(3):
                row = 256 * (3 * kh + kw)
                x9[row : row + 256, 128 * j : 128 * j + 128] = tile[:, 128 * kw : 128 * kw + 128]
    grads = dot_t(c3[:, 128:640], x9[...])
    rsg[0:32, 0:2304] = grads[0:32]
    rsg[0:32, 2304:3456] = grads[32:64, 0:1152]
    rsg[32:64, 0:1152] = grads[32:64, 1152:2304]
    rsg[32:64, 1152:3456] = grads[64:96]
    rsg[:, 3456:3584] = jnp.zeros((64, 128), F32)
    for k in range(32):
        piece = rsg[:, 108 * k : 108 * k + 128].astype(BF16)
        ts[k % 2, (k % 8) // 2, k // 8] = piece[0:32]
        ts[k % 2, (k % 8) // 2, k // 8 + 4] = piece[32:64]
    send(S_KS, ts.at[1 - core], cs, kdev)

    recv(S_KS, cs, kdev)
    us[...] = (ts[core].astype(F32) + cs[...].astype(F32)).astype(BF16)
    for k in (1, 0, 2):
        send(S_YS + k, us.at[lax.rem(y + k + 1, NY)], yg.at[k], ydev[k])

    out = dot(w2s[...], x9[...])
    ys[0:32] = out[0:32].astype(BF16)
    ys[32:64] = out[64:96].astype(BF16)

    total = uf[y].astype(F32)
    for k in range(3):
        recv(S_YF + k, yf.at[k], ydev[2 - k])
        total = total + yf[k].astype(F32)
    vf[...] = total.astype(BF16)
    for k in range(7):
        send(S_ZF + k, vf.at[lax.rem(zl + k + 1, 4)], zf.at[k], zldev[k])

    total = us[y].astype(F32)
    for k in range(3):
        recv(S_YS + k, yg.at[k], ydev[2 - k])
        total = total + yg[k].astype(F32)
    vs[...] = total.astype(BF16)
    for k in range(7):
        send(S_ZS + k, vs.at[lax.rem(zl + k + 1, NZ)], zs.at[k], zldev[k])

    send(S_Y, ys.at[0:32], yr.at[0], up, jnp.logical_not(last))
    send(S_Y + 1, ys.at[32:64], yr.at[1], down, jnp.logical_not(first))
    recv(S_Y, yr.at[0], down, jnp.logical_not(first))
    recv(S_Y + 1, yr.at[1], up, jnp.logical_not(last))
    before = jnp.where(first, 0.0, yr[0].astype(F32))
    after = jnp.where(last, 0.0, yr[1].astype(F32))
    rounded = (out[32:64] + before + after).astype(BF16)
    lines = jnp.concatenate([rounded[:, 64 * h : 64 * h + 64] for h in range(8)], axis=0)
    so[:, 0] = dot(swap_matrix(256, 8), lines).reshape(32, 8, 64).astype(BF16)

    total = vf[lax.rem(zl, 4)].astype(F32)
    for k in range(7):
        recv(S_ZF + k, zf.at[k], zldev[6 - k])
        total = total + zf[k].astype(F32)
    fgo[...] = jnp.where(zl < 4, total[:, 0:54], total[:, 64:118])
    total = vs[zl].astype(F32)
    for k in range(7):
        recv(S_ZS + k, zs.at[k], zldev[6 - k])
        total = total + zs[k].astype(F32)
    sgo[...] = total[:, 0:108]

    for copy, cond in pending:
        if cond is None:
            copy.wait_send()
        else:
            pl.when(cond)(copy.wait_send)


def shards(sample, first_weight, second_weight, cotangent):
    vmem = pl.BlockSpec(memory_space=pltpu.VMEM)
    hbm = pl.BlockSpec(memory_space=pltpu.HBM)
    b16 = [
        (16, 2, 16, 128), (32, 3456), (32, 6912), (32, 1, 8, 64), (32, 16, 128), (32, 512), (33, 128, 128),
        (2, 1152, 512), (96, 768), (864, 512), (864, 256),
    ]
    scratch = [pltpu.VMEM(shape, BF16) for shape in b16]
    scratch += [pltpu.VMEM((256, 512), F32)]
    scratch += [pltpu.VMEM((256, 512), BF16), pltpu.VMEM((3, 64, 512), BF16), pltpu.VMEM((64, 512), F32)]
    scratch += [pltpu.VMEM((64, 512), BF16), pltpu.VMEM((32, 512), BF16)]
    scratch += [pltpu.VMEM((4, 2, 7, 16, 128), BF16)] * 2
    scratch += [pltpu.VMEM((128, 1152), BF16), pltpu.VMEM((64, 1152), BF16)]
    scratch += [pltpu.VMEM((64, 512), F32)] * 3
    scratch += [pltpu.VMEM(shape, BF16) for shape in ((256, 768), (64, 512), (2304, 512), (96, 2304), (64, 512), (2, 32, 512))]
    scratch += [pltpu.VMEM((64, 3584), F32), pltpu.VMEM((32, 3584), F32)]
    for n in (4, 8):
        shapes = ((2, 4, n), (4, n), (4, n), (3, n), (n,), (7,))
        scratch += [pltpu.VMEM(shape + (32, 128), BF16) for shape in shapes]
    scratch += [pltpu.SemaphoreType.DMA((N_SEM,))] * 2 + [pltpu.SemaphoreType.DMA((4,))]
    so, fgo, sgo = pl.pallas_call(
        kernel,
        out_shape=(
            jax.ShapeDtypeStruct((32, 1, 8, 64), BF16),
            jax.ShapeDtypeStruct((32, 54), F32),
            jax.ShapeDtypeStruct((32, 108), F32),
        ),
        in_specs=[hbm] * 4,
        out_specs=(vmem, vmem, vmem),
        scratch_shapes=scratch,
        compiler_params=pltpu.CompilerParams(collective_id=0, has_side_effects=True, vmem_limit_bytes=VMEM_BYTES),
        name="slab_pair",
    )(sample, first_weight, second_weight, cotangent)
    return so, fgo, sgo


def solution(mesh):
    return jax.shard_map(
        shards,
        mesh=mesh,
        in_specs=(
            P("chan", "depth", None, None),
            P("chan", None),
            P("chan", None),
            P("chan", "depth", None, None),
        ),
        out_specs=(P("chan", "depth", None, None), P("chan", "depth"), P("chan", "depth")),
        check_vma=False,
    )
```

```python
import jax
import jax.numpy as jnp
from jax import lax
from jax.experimental import pallas as pl
from jax.experimental.pallas import tpu as pltpu
from jax.sharding import PartitionSpec as P

LEAK = 0.3
F32 = jnp.float32
BF16 = jnp.bfloat16
MESH = pl.DeviceIdType.MESH

NZ, NY, NK, NX = 8, 4, 2, 4
DEPTH = NZ * NY * NK

S_Z = 0
S_OX = 3
S_FX = 9
S_ACT = 18
S_COT = 21
S_AGX = 23
S_AGZ = 26
S_B1 = 27
S_PG = 28
S_Y = 29
S_KF = 31
S_KS = 32
S_YF = 33
S_YS = 36
S_ZF = 39
S_ZS = 46
S_WZ = 53
S_WY = 54
S_WK = 57
N_SEM = 58

VMEM_BYTES = 64 * 1024 * 1024 - 16 * 1024

CHUNKS = ((16, 32), (7, 16), (0, 7))


def dot(a, b):
    return lax.dot_general(a, b, (((1,), (0,)), ((), ())), preferred_element_type=F32)


def dot_t(a, b):
    return lax.dot_general(a, b, (((1,), (1,)), ((), ())), preferred_element_type=F32)


def shift_matrix(rows, base):
    r = lax.broadcasted_iota(jnp.int32, (rows, 384), 0)
    c = lax.broadcasted_iota(jnp.int32, (rows, 384), 1)
    kw = c >> 7
    m = c & 127
    w = (m & 63) + kw - 1
    hit = (r == m + base + kw - 1) & (w >= 0) & (w < 64)
    return jnp.where(hit, 1.0, 0.0).astype(BF16)


def stride_matrix():
    r = lax.broadcasted_iota(jnp.int32, (256, 384), 0)
    c = lax.broadcasted_iota(jnp.int32, (256, 384), 1)
    kw = c >> 7
    i = (c >> 6) & 1
    w = 2 * (c & 63) + kw - 1
    hit = (r == i * 128 + w) & (w >= 0)
    return jnp.where(hit, 1.0, 0.0).astype(BF16)


def swap_matrix(rows, fast):
    slow = rows // fast
    bits = slow.bit_length() - 1
    r = lax.broadcasted_iota(jnp.int32, (rows, rows), 0)
    k = lax.broadcasted_iota(jnp.int32, (rows, rows), 1)
    hit = ((k >> bits) == (r & (fast - 1))) & ((k & (slow - 1)) == (r >> (fast.bit_length() - 1)))
    return jnp.where(hit, 1.0, 0.0).astype(BF16)


def kernel(
    samp_hbm, w1_hbm, w2_hbm, cot_hbm,
    so, fgo, sgo,
    sraw, w1, w2, craw, own, cot, g, s, c3, ci, wv, ag32, agb, agr, az32, azb, azr, wo, wp, w1p, w1m, b1s, b1r,
    slope, act, pg2, x9, w2s, ys, yr, rsg, rfg, tf, cf, uf, yf, vf, zf, ts, cs, us, yg, vs, zs,
    send_sems, recv_sems, load_sems,
):
    d = lax.axis_index("depth")
    c = lax.axis_index("chan")
    core = lax.rem(d, 2)
    y = lax.rem(d // 2, NY)
    zl = d // (2 * NY)
    x = c // 2
    zh = lax.rem(c, 2)
    first = d == 0
    last = d == DEPTH - 1

    def chan_at(dx, flip=False):
        return lax.rem(x + dx + NX, NX) * 2 + (1 - zh if flip else zh)

    xdev = [(d, chan_at(k)) for k in (1, 2, 3)]
    zdev = (d, chan_at(0, True))
    kdev = (d + 1 - 2 * core, c)
    ydev = [(zl * 8 + lax.rem(y + k, NY) * 2 + core, c) for k in (1, 2, 3)]
    zldev = [(lax.rem(zl + k, NZ) * 8 + y * 2 + core, c) for k in range(1, 8)]
    up = (lax.rem(d + 1, DEPTH), c)
    down = (lax.rem(d + DEPTH - 1, DEPTH), c)

    barrier = pltpu.get_barrier_semaphore()
    partners = [zdev] + zldev + xdev + ydev + [kdev, up, down]
    for dev in partners:
        pl.semaphore_signal(barrier, inc=1, device_id=dev, device_id_type=MESH)
    loads = [
        pltpu.make_async_copy(src, dst, load_sems.at[i])
        for i, (src, dst) in enumerate(((samp_hbm, sraw), (cot_hbm, craw), (w1_hbm, w1), (w2_hbm, w2)))
    ]
    for load in loads:
        load.start()

    pending = []

    def desc(k, src, dst, dev):
        return pltpu.make_async_remote_copy(
            src_ref=src, dst_ref=dst, send_sem=send_sems.at[k], recv_sem=recv_sems.at[k], device_id=dev, device_id_type=MESH
        )

    def send(k, src, dst, dev, cond=None):
        copy = desc(k, src, dst, dev)
        if cond is None:
            copy.start()
        else:
            pl.when(cond)(copy.start)
        pending.append((copy, cond))

    def recv(k, dst, dev, cond=None):
        copy = desc(k, dst, dst, dev)
        if cond is None:
            copy.wait_recv()
        else:
            pl.when(cond)(copy.wait_recv)

    def rows(start, size):
        return pl.ds(pl.multiple_of(start, size), size)

    def sample_block(r, lines):
        return g.at[lines[0] : lines[1], rows(r * 16, 16), :]

    loads[0].wait()
    swap = swap_matrix(256, 16)
    for plane in range(2):
        lines = dot(swap, sraw[:, plane].reshape(256, 128))
        own[16 * plane : 16 * plane + 16] = lines.astype(BF16).reshape(16, 16, 128)
    loads[1].wait()
    lines = dot(swap_matrix(256, 32), craw[:, 0].astype(F32).reshape(256, 64).astype(BF16))
    for j in range(4):
        pair = jnp.concatenate([lines[64 * j : 64 * j + 32], lines[64 * j + 32 : 64 * j + 64]], axis=1)
        cot[:, 128 * j : 128 * j + 128] = pair.astype(BF16)
    loads[2].wait()
    wo[3, 1] = jnp.zeros((7, 16, 128), BF16)
    for k in range(54):
        at = 16 * (k % 2)
        wo[k // 14, k // 7 % 2, k % 7] = w1[at : at + 16, 128 * (k // 2) : 128 * (k // 2) + 128]
    pl.semaphore_wait(barrier, len(partners))

    filt = desc(S_WZ, wo.at[y, core], wp.at[y, core], zdev)
    filt.start()
    over = [desc(S_Z + i, own.at[a:b], sample_block(c, (a, b)), zdev) for i, (a, b) in enumerate(CHUNKS)]
    send(S_COT, cot, c3.at[64:96, 128:640], up, jnp.logical_not(last))
    send(S_COT + 1, cot, c3.at[0:32, 128:640], down, jnp.logical_not(first))
    for i, lines in enumerate(((16, 32), (0, 16))):
        for k in (1, 0, 2):
            send(S_OX + 3 * i + k, own.at[lines[0] : lines[1]], sample_block(c, lines), xdev[k])

    filt.wait_send()
    over[0].start()
    c3[:, 0:128] = jnp.zeros((96, 128), BF16)
    c3[:, 640:768] = jnp.zeros((96, 128), BF16)
    act[:, 0:128] = jnp.zeros((256, 128), BF16)
    act[:, 640:768] = jnp.zeros((256, 128), BF16)
    g[32] = jnp.zeros((128, 128), BF16)

    @pl.when(first)
    def _():
        c3[64:96, 128:640] = jnp.zeros((32, 512), BF16)

    @pl.when(last)
    def _():
        c3[0:32, 128:640] = jnp.zeros((32, 512), BF16)
        pg2[32:64] = jnp.zeros((32, 512), BF16)

    c3[32:64, 128:640] = cot[...]
    g[0:32, rows(c * 16, 16), :] = own[...]
    loads[3].wait()
    for k in range(27):
        wv[32 * k : 32 * k + 32] = w2[:, 256 * k : 256 * k + 256]
    for k in range(3):
        w2s[32 * k : 32 * k + 32] = w2[:, 2304 * k : 2304 * k + 2304]
    mine = pl.multiple_of(zh * 32, 32)
    theirs = pl.multiple_of((1 - zh) * 32, 32)
    w1p[pl.ds(mine, 32)] = w1[:, 2304:3456]
    w1p[pl.ds(mine + 64, 32)] = w1[:, 0:1152]
    w1m[pl.ds(mine, 32)] = w1[:, 1152:2304]
    sh_two = shift_matrix(256, 64)
    sh_one = shift_matrix(128, 0)
    recv(S_COT, c3.at[64:96, 128:640], down, jnp.logical_not(first))
    recv(S_COT + 1, c3.at[0:32, 128:640], up, jnp.logical_not(last))

    def shifted(ref, j, kh):
        if kh == 1:
            return dot(ref[:, 128 * (j + 1) : 128 * (j + 2)], sh_one).astype(BF16)
        at = 128 * j if kh == 0 else 128 * (j + 1)
        return dot(ref[:, at : at + 256], sh_two).astype(BF16)

    for j in range(4):
        for kh in range(3):
            tile = shifted(c3, j, kh)
            for kw in range(3):
                for kd in range(3):
                    tap = 9 * kd + 3 * (2 - kh) + 2 - kw
                    ci[32 * tap : 32 * tap + 32, 128 * j : 128 * j + 128] = tile[32 * kd : 32 * kd + 32, 128 * kw : 128 * kw + 128]
    part = lax.dot_general(wv[...], ci[...], (((0,), (0,)), ((), ())), preferred_element_type=F32)
    ag32[...] = part
    agb[...] = part.astype(BF16)
    for k in (1, 0, 2):
        send(S_AGX + k, agb.at[rows(lax.rem(x + k + 1, NX) * 64, 64)], agr.at[k], xdev[k])

    over[0].wait_send()
    over[1].start()
    recv(S_WZ, wp.at[y, core], zdev)
    for k in range(3):
        send(S_WY + k, wp.at[y, core], wp.at[y, core], ydev[k])

    over[1].wait_send()
    over[2].start()
    total = ag32[rows(x * 64, 64)]
    for k in range(3):
        recv(S_AGX + k, agr.at[k], xdev[2 - k])
        total = total + agr[k].astype(F32)
    az32[...] = total
    azb[...] = total.astype(BF16)
    over[2].wait_send()
    send(S_AGZ, azb.at[pl.ds(theirs, 32)], azr, zdev)

    def across(i):
        block = sample_block(chan_at(0, True), CHUNKS[i])
        recv(S_Z + i, block, zdev)
        for k in (1, 0, 2):
            send(S_FX + 3 * i + k, block, block, xdev[k])

    def arrived(i):
        for k in range(3):
            recv(S_FX + 3 * i + k, sample_block(chan_at(3 - k, True), CHUNKS[i]), xdev[2 - k])

    across(0)
    for k in range(3):
        recv(S_WY + k, wp.at[lax.rem(y + 3 - k, NY), core], ydev[2 - k])
    send(S_WK, wp.at[:, core], wp.at[:, core], kdev)
    across(1)
    for i, lines in enumerate(((16, 32), (0, 16))):
        for k in range(3):
            recv(S_OX + 3 * i + k, sample_block(chan_at(3 - k), lines), xdev[2 - k])
    stride = stride_matrix()

    def strided(plane, j):
        for kh in range(3):
            at = 4 * j + kh - 1
            low = g[16 * plane + at] if at >= 0 else g[32]
            tile = dot(jnp.concatenate([low, g[16 * plane + at + 2]], axis=1), stride).astype(BF16)
            for kw in range(3):
                row = 128 * (3 * kh + kw)
                s[plane, row : row + 128, 128 * j : 128 * j + 128] = tile[:, 128 * kw : 128 * kw + 128]

    arrived(0)
    for j in range(4):
        strided(1, j)
    recv(S_WK, wp.at[:, 1 - core], kdev)
    for k in range(54):
        tile = wp[k // 14, k // 7 % 2, k % 7]
        at = 128 * (k // 2 % 9)
        row = theirs + 16 * (k % 2)
        if k // 18 == 1:
            w1m[pl.ds(row, 16), at : at + 128] = tile
        else:
            w1p[pl.ds(row + (64 if k < 18 else 0), 16), at : at + 128] = tile
    both = dot(w1p[...], s[1])
    b1s[...] = both[64:128]
    send(S_B1, b1s, b1r, up, jnp.logical_not(last))
    across(2)
    arrived(1)
    halves = [None, None]
    for half in (1, 0):
        if half == 0:
            arrived(2)
        strided(0, 2 * half)
        strided(0, 2 * half + 1)
        halves[half] = dot(w1m[...], s[0, :, 256 * half : 256 * half + 256])
    pre = both[0:64] + jnp.concatenate(halves, axis=1)
    recv(S_B1, b1r, down, jnp.logical_not(first))
    pre = pre + jnp.where(first, 0.0, b1r[...])
    sl = jnp.where(pre > 0, 1.0, LEAK)
    group = act.at[rows(x * 64, 64), 128:640]
    group[...] = (pre * sl).astype(BF16)
    for k in (1, 0, 2):
        send(S_ACT + k, group, group, xdev[k])
    slope[...] = sl

    recv(S_AGZ, azr, zdev)
    grad = az32[pl.ds(mine, 32)] + azr[...].astype(F32)
    pg2[0:32] = (grad * slope[pl.ds(mine, 32)]).astype(BF16)
    send(S_PG, pg2.at[0:32], pg2.at[32:64], down, jnp.logical_not(first))
    rfg[:, 1152:2304] = dot_t(pg2[0:32], s[0])
    rfg[:, 3456:3584] = jnp.zeros((32, 128), F32)
    recv(S_PG, pg2.at[32:64], up, jnp.logical_not(last))
    both = dot_t(pg2[...], s[1])
    rfg[:, 2304:3456] = both[0:32]
    rfg[:, 0:1152] = both[32:64]

    for k in range(32):
        low = rfg[:, 54 * k : 54 * k + 64]
        high = rfg[:, 54 * (k + 32) : 54 * (k + 32) + 64]
        tf[k % 2, (k % 8) // 2, k // 8] = jnp.concatenate([low, high], axis=1).astype(BF16)
    send(S_KF, tf.at[1 - core], cf, kdev)

    for k in range(3):
        recv(S_ACT + k, act.at[rows(lax.rem(x + 3 - k, NX) * 64, 64), 128:640], xdev[2 - k])
    recv(S_KF, cf, kdev)
    uf[...] = (tf[core].astype(F32) + cf[...].astype(F32)).astype(BF16)
    for k in (1, 0, 2):
        send(S_YF + k, uf.at[lax.rem(y + k + 1, NY)], yf.at[k], ydev[k])
    for j in range(4):
        for kh in range(3):
            tile = shifted(act, j, kh)
            for kw in range(3):
                row = 256 * (3 * kh + kw)
                x9[row : row + 256, 128 * j : 128 * j + 128] = tile[:, 128 * kw : 128 * kw + 128]
    grads = dot_t(c3[:, 128:640], x9[...])
    rsg[0:32, 0:2304] = grads[0:32]
    rsg[0:32, 2304:3456] = grads[32:64, 0:1152]
    rsg[32:64, 0:1152] = grads[32:64, 1152:2304]
    rsg[32:64, 1152:3456] = grads[64:96]
    rsg[:, 3456:3584] = jnp.zeros((64, 128), F32)
    for k in range(32):
        piece = rsg[:, 108 * k : 108 * k + 128].astype(BF16)
        ts[k % 2, (k % 8) // 2, k // 8] = piece[0:32]
        ts[k % 2, (k % 8) // 2, k // 8 + 4] = piece[32:64]
    send(S_KS, ts.at[1 - core], cs, kdev)

    recv(S_KS, cs, kdev)
    us[...] = (ts[core].astype(F32) + cs[...].astype(F32)).astype(BF16)
    for k in (1, 0, 2):
        send(S_YS + k, us.at[lax.rem(y + k + 1, NY)], yg.at[k], ydev[k])

    out = dot(w2s[...], x9[...])
    ys[0:32] = out[0:32].astype(BF16)
    ys[32:64] = out[64:96].astype(BF16)

    total = uf[y].astype(F32)
    for k in range(3):
        recv(S_YF + k, yf.at[k], ydev[2 - k])
        total = total + yf[k].astype(F32)
    vf[...] = total.astype(BF16)
    for k in range(7):
        send(S_ZF + k, vf.at[lax.rem(zl + k + 1, 4)], zf.at[k], zldev[k])

    total = us[y].astype(F32)
    for k in range(3):
        recv(S_YS + k, yg.at[k], ydev[2 - k])
        total = total + yg[k].astype(F32)
    vs[...] = total.astype(BF16)
    for k in range(7):
        send(S_ZS + k, vs.at[lax.rem(zl + k + 1, NZ)], zs.at[k], zldev[k])

    send(S_Y, ys.at[0:32], yr.at[0], up, jnp.logical_not(last))
    send(S_Y + 1, ys.at[32:64], yr.at[1], down, jnp.logical_not(first))
    recv(S_Y, yr.at[0], down, jnp.logical_not(first))
    recv(S_Y + 1, yr.at[1], up, jnp.logical_not(last))
    before = jnp.where(first, 0.0, yr[0].astype(F32))
    after = jnp.where(last, 0.0, yr[1].astype(F32))
    rounded = (out[32:64] + before + after).astype(BF16)
    lines = jnp.concatenate([rounded[:, 64 * h : 64 * h + 64] for h in range(8)], axis=0)
    so[:, 0] = dot(swap_matrix(256, 8), lines).reshape(32, 8, 64).astype(BF16)

    total = vf[lax.rem(zl, 4)].astype(F32)
    for k in range(7):
        recv(S_ZF + k, zf.at[k], zldev[6 - k])
        total = total + zf[k].astype(F32)
    fgo[...] = jnp.where(zl < 4, total[:, 0:54], total[:, 64:118])
    total = vs[zl].astype(F32)
    for k in range(7):
        recv(S_ZS + k, zs.at[k], zldev[6 - k])
        total = total + zs[k].astype(F32)
    sgo[...] = total[:, 0:108]

    for copy, cond in pending:
        if cond is None:
            copy.wait_send()
        else:
            pl.when(cond)(copy.wait_send)


def shards(sample, first_weight, second_weight, cotangent):
    vmem = pl.BlockSpec(memory_space=pltpu.VMEM)
    hbm = pl.BlockSpec(memory_space=pltpu.HBM)
    b16 = [
        (16, 2, 16, 128), (32, 3456), (32, 6912), (32, 1, 8, 64), (32, 16, 128), (32, 512), (33, 128, 128),
        (2, 1152, 512), (96, 768), (864, 512), (864, 256),
    ]
    scratch = [pltpu.VMEM(shape, BF16) for shape in b16]
    scratch += [pltpu.VMEM((256, 512), F32)]
    scratch += [pltpu.VMEM((256, 512), BF16), pltpu.VMEM((3, 64, 512), BF16), pltpu.VMEM((64, 512), F32)]
    scratch += [pltpu.VMEM((64, 512), BF16), pltpu.VMEM((32, 512), BF16)]
    scratch += [pltpu.VMEM((4, 2, 7, 16, 128), BF16)] * 2
    scratch += [pltpu.VMEM((128, 1152), BF16), pltpu.VMEM((64, 1152), BF16)]
    scratch += [pltpu.VMEM((64, 512), F32)] * 3
    scratch += [pltpu.VMEM(shape, BF16) for shape in ((256, 768), (64, 512), (2304, 512), (96, 2304), (64, 512), (2, 32, 512))]
    scratch += [pltpu.VMEM((64, 3584), F32), pltpu.VMEM((32, 3584), F32)]
    for n in (4, 8):
        shapes = ((2, 4, n), (4, n), (4, n), (3, n), (n,), (7,))
        scratch += [pltpu.VMEM(shape + (32, 128), BF16) for shape in shapes]
    scratch += [pltpu.SemaphoreType.DMA((N_SEM,))] * 2 + [pltpu.SemaphoreType.DMA((4,))]
    so, fgo, sgo = pl.pallas_call(
        kernel,
        out_shape=(
            jax.ShapeDtypeStruct((32, 1, 8, 64), BF16),
            jax.ShapeDtypeStruct((32, 54), F32),
            jax.ShapeDtypeStruct((32, 108), F32),
        ),
        in_specs=[hbm] * 4,
        out_specs=(vmem, vmem, vmem),
        scratch_shapes=scratch,
        compiler_params=pltpu.CompilerParams(collective_id=0, has_side_effects=True, vmem_limit_bytes=VMEM_BYTES),
        name="slab_pair",
    )(sample, first_weight, second_weight, cotangent)
    return so, fgo, sgo


def solution(mesh):
    return jax.shard_map(
        shards,
        mesh=mesh,
        in_specs=(
            P("chan", "depth", None, None),
            P("chan", None),
            P("chan", None),
            P("chan", "depth", None, None),
        ),
        out_specs=(P("chan", "depth", None, None), P("chan", "depth"), P("chan", "depth")),
        check_vma=False,
    )
```
